128 devices in a mesh: expert: 16 (over x, y), tensor: 8 (over z, core).
Axes of the slice: x: 4, y: 4, z: 4, core: 2. Of those that a mesh axis runs over, the one named last changes fastest.
Arguments:
- layer_input: bfloat16 [16384, 1024], P(('expert', 'tensor')), may hold values from -6 to 6
- routes: int32 [16384, 8], P(('expert', 'tensor')), may hold values from 0 to 31, all different within a row; in each aligned block of 128 rows (0 to 127, 128 to 255, ...) at most 48 rows name the same one
- cotangent: bfloat16 [16384, 1024], P(('expert', 'tensor')), may hold values from -6 to 6
- gain_attn: float32 [1024], replicated, may hold values from 0.5 to 1.5
- gain_moe: float32 [1024], replicated, may hold values from 0.5 to 1.5
- w_query: bfloat16 [1024, 1024], P(None, 'tensor'), may hold values from -0.1875 to 0.1875
- w_key: bfloat16 [1024, 512], P(None, 'tensor'), may hold values from -0.1875 to 0.1875
- w_value: bfloat16 [1024, 512], P(None, 'tensor'), may hold values from -0.1875 to 0.1875
- w_out: bfloat16 [1024, 1024], P('tensor'), may hold values from -0.75 to 0.75
- w_router: bfloat16 [1024, 32], replicated, may hold values from -0.09375 to 0.09375
- w_gate: bfloat16 [32, 1024, 512], P('expert', None, 'tensor'), may hold values from -0.1875 to 0.1875
- w_up: bfloat16 [32, 1024, 512], P('expert', None, 'tensor'), may hold values from -0.1875 to 0.1875
- w_down: bfloat16 [32, 512, 1024], P('expert', 'tensor'), may hold values from -0.75 to 0.75
Outputs:
- output: bfloat16 [16384, 1024], P(('expert', 'tensor'))
- grad_input: float32 [16384, 1024], P(('expert', 'tensor'))
- grad_query: float32 [1024, 1024], P(None, 'tensor')
- grad_key: float32 [1024, 512], P(None, 'tensor')
- grad_value: float32 [1024, 512], P(None, 'tensor')
- grad_out: float32 [1024, 1024], P('tensor')
- grad_gain_attn: float32 [1024], replicated
- grad_gain_moe: float32 [1024], replicated
- grad_router: float32 [1024, 32], replicated
- grad_gate: float32 [32, 1024, 512], P('expert', None, 'tensor')
- grad_up: float32 [32, 1024, 512], P('expert', None, 'tensor')
- grad_down: float32 [32, 512, 1024], P('expert', 'tensor')
The draws below stay inside these ranges and needn't reach their ends.
Inputs may be any that keep to these rules, and one draw needn't show every extreme that they name: `routes`: each row names 8 different experts. In each aligned block of 128 rows (the rows of one device) no expert is named by more than 48 rows, and in some block one expert is named by exactly 48 rows.
All inputs are finite; a program needn't handle non-finite values.
Results may differ from the reference program's by a relative error of at most 0.024.
Values may be sent and summed in bfloat16 or wider, within the bound.
A program may use at most 128 MiB of HBM per device.

```python
import math
import jax
import jax.numpy as jnp
import numpy as np
from jax import lax

D = 1024
HEADS = 16
KV_HEADS = 8
HEAD_DIM = 64
EXPERTS = 32
TOP = 8
FFE = 512
TOK_DEV = 128
SEQ = 1024
TOKENS = 16384
CAP = 48
N_EXPERT = 16


def level_of(own_key, extent, pieces, smallest, high):
    loudness, own = 1.0, jax.random.fold_in(own_key, 6)
    for dim, shards_of in pieces:
        draws = jnp.exp(jax.random.uniform(jax.random.fold_in(own, dim), (shards_of,), jnp.float32, smallest / len(pieces), high / len(pieces)))
        loudness = loudness * jnp.repeat(draws, extent[dim] // shards_of).reshape([-1 if axis == dim else 1 for axis in range(len(extent))])
    return loudness


def routed_block(rng, own, number, rows, count, top, most, lean):
    order = jax.random.permutation(rng, count)
    crowded, common = shares(count, rows * top, most, lean, True), shares(count, rows * top, most, lean, False)
    places = jnp.arange(count)

    def named(sizes, turn):
        used = int((sizes > 0).sum())
        fixed = max(1, used // 4)
        shifted = fixed + (places - fixed + turn * (used - fixed)) % max(1, count - fixed)
        return jnp.zeros((count,), jnp.int32).at[order[jnp.where(places < fixed, places, shifted)]].set(jnp.asarray(sizes, jnp.int32))

    sizes = jnp.where(number % 4 == 0, named(crowded, number // 4), named(common, number - number // 4 - 1))
    mixed = jax.random.permutation(jax.random.fold_in(own, 3), count)
    giver, sink = mixed[0:count // 2 * 2:2], mixed[1:count // 2 * 2:2]
    margin = jnp.minimum(sizes[giver] - 1, most - sizes[sink]) // 2
    margin = jnp.where((giver == order[0]) | (sink == order[0]) | (sizes[sink] == 0), 0, jnp.maximum(margin, 0))
    shifted = jax.random.randint(jax.random.fold_in(own, 4), (count // 2,), 0, 1 << 20) % (margin + 1)
    sizes = sizes.at[giver].add(-shifted).at[sink].add(shifted)
    members = jnp.searchsorted(jnp.cumsum(sizes), jnp.arange(rows * top), side="right").astype(jnp.int32)
    table = members.reshape(top, rows).T
    table = table[jax.random.permutation(jax.random.fold_in(own, 1), rows)]
    turn = jax.random.randint(jax.random.fold_in(own, 2), (rows, 1), 0, top)
    return jnp.take_along_axis(table, (jnp.arange(top)[None, :] + turn) % top, axis=1)


def shares(number_of, total, most, lean, full):
    loads = [(1 << 20) // math.isqrt(rank ** lean) + 1 for rank in range(1, number_of + 1)]
    largest = most if full else min(most, max(-(-total // number_of), total * loads[0] // sum(loads)))
    least = 1 if total - largest >= number_of - 1 else 0
    holding, rest = [largest] + [least] * (number_of - 1), total - largest - least * (number_of - 1)
    while rest > 0:
        candidates = [i for i in range(1, number_of) if holding[i] < largest] or [i for i in range(1, number_of) if holding[i] < most]
        mass, left = sum([loads[i] for i in candidates]), rest
        for i in candidates:
            extra = min(most - holding[i], max(1, left * loads[i] // mass), rest)
            holding[i] = holding[i] + extra
            rest = rest - extra
    return np.array(holding)


def centred(key, shape, spread, most, cuts=(), kind=jnp.bfloat16):
    values = jax.random.normal(key, shape, jnp.float32) * spread
    if len(cuts) > 0:
        values = level_of(key, shape, cuts, -0.22, 0.18) * values
    return jnp.clip(values, min=-most, max=most).astype(kind)


def setup_inputs(seed: int = 0) -> dict:
    splits = jax.random.split(jax.random.key(seed), 14)
    layer_input = centred(splits[0], (TOKENS, D), 1.0, 6.0, ((0, 128),))
    routes_keys = jax.random.split(jax.random.fold_in(splits[1], 1), TOKENS // TOK_DEV)
    routes_turns = jax.random.permutation(jax.random.fold_in(splits[1], 3), TOKENS // TOK_DEV)
    routes = jax.vmap(lambda own, number: routed_block(jax.random.fold_in(splits[1], 2), own, number, TOK_DEV, EXPERTS, TOP, CAP, 1))(routes_keys, routes_turns).reshape((TOKENS, TOP))
    cotangent = centred(splits[2], (TOKENS, D), 1.0, 6.0, ((0, 128),))
    gain_attn = jnp.clip(1.0 + 0.1 * jax.random.normal(splits[3], (D,), jnp.float32), 0.5, 1.5)
    gain_moe = jnp.clip(1.0 + 0.1 * jax.random.normal(splits[4], (D,), jnp.float32), 0.5, 1.5)
    w_query = centred(splits[5], (D, HEADS * HEAD_DIM), D ** -0.5, 0.1875, ((1, 8),))
    w_key = centred(splits[6], (D, KV_HEADS * HEAD_DIM), D ** -0.5, 0.1875, ((1, 8),))
    w_value = centred(splits[7], (D, KV_HEADS * HEAD_DIM), D ** -0.5, 0.1875, ((1, 8),))
    w_out = centred(splits[8], (HEADS * HEAD_DIM, D), (HEADS * HEAD_DIM // 16) ** -0.5, 0.75, ((0, 8),))
    w_router = centred(splits[9], (D, EXPERTS), (4 * D) ** -0.5, 0.09375)
    w_gate = centred(splits[10], (EXPERTS, D, FFE), D ** -0.5, 0.1875, ((0, 16), (2, 8)))
    w_up = centred(splits[11], (EXPERTS, D, FFE), D ** -0.5, 0.1875, ((0, 16), (2, 8)))
    w_down = centred(splits[12], (EXPERTS, FFE, D), (FFE // 9) ** -0.5, 0.75, ((0, 16), (1, 8)))
    return {"layer_input": layer_input, "routes": routes, "cotangent": cotangent, "gain_attn": gain_attn, "gain_moe": gain_moe, "w_query": w_query, "w_key": w_key, "w_value": w_value, "w_out": w_out, "w_router": w_router, "w_gate": w_gate, "w_up": w_up, "w_down": w_down}


EPS = 1e-06
THETA = 10000.0
HIGH = lax.Precision.HIGHEST

@jax.custom_vjp
def low(v):
    return lax.optimization_barrier(v.astype(jnp.bfloat16)).astype(jnp.float32)

@jax.custom_vjp
def low_back(v):
    return v

def low_keep(v):
    return (low(v), None)

def low_pass(kept, grad):
    return (grad,)

def back_keep(v):
    return (v, None)

def back_low(kept, grad):
    return (low(grad),)
low.defvjp(low_keep, low_pass)
low_back.defvjp(back_keep, back_low)

def rms_scale(values, gain):
    return values * lax.rsqrt(lax.optimization_barrier(jnp.mean(values * values, -1, keepdims=True)) + EPS) * gain

def rotate(values, positions):
    half = values.shape[-1] // 2
    freqs = THETA ** (-jnp.arange(half, dtype=jnp.float32) * 2.0 / values.shape[-1])
    angles = positions.astype(jnp.float32)[:, None] * freqs[None, :]
    cosine = jnp.cos(angles)[:, None, :]
    sine = jnp.sin(angles)[:, None, :]
    first = values[..., :half]
    second = values[..., half:]
    return jnp.concatenate([first * cosine - second * sine, second * cosine + first * sine], -1)

def attend(query, keys, values):
    share = query.shape[1] // keys.shape[1]
    keys_all = jnp.repeat(keys, share, axis=1)
    values_all = jnp.repeat(values, share, axis=1)
    raw = jnp.einsum('qhd,khd->hqk', query, keys_all, precision=HIGH) * query.shape[-1] ** (-0.5)
    scores = low_back(raw)
    places = jnp.arange(query.shape[0], dtype=jnp.int32)
    causal = places[None, :] <= places[:, None]
    scores = jnp.where(causal[None], scores, -1e+30)
    probs = low(jax.nn.softmax(scores, axis=-1))
    return jnp.einsum('hqk,khd->qhd', probs, values_all, precision=HIGH)

def make_tables(routes):
    expert_ids = routes.reshape(-1).astype(jnp.int32)
    count = expert_ids.shape[0]
    per_dev = TOK_DEV * TOP
    devices = count // per_dev
    hot = (expert_ids[:, None] == jnp.arange(EXPERTS, dtype=jnp.int32)[None, :]).astype(jnp.int32)
    ranks = jnp.cumsum(hot.reshape(devices, per_dev, EXPERTS), axis=1).astype(jnp.int32).reshape(count, EXPERTS)
    slot = lax.optimization_barrier(jnp.sum(ranks * hot, axis=1)).astype(jnp.int32) - 1
    device = jnp.arange(count, dtype=jnp.int32) // per_dev
    token = jnp.arange(count, dtype=jnp.int32) // TOP
    cells = (expert_ids * devices + device) * CAP + slot
    total = EXPERTS * devices * CAP
    token_of = jnp.zeros((total,), jnp.int32).at[cells].set(token)
    source_of = jnp.zeros((total,), jnp.int32).at[cells].set(jnp.arange(count, dtype=jnp.int32))
    used = jnp.zeros((total,), jnp.int32).at[cells].set(1)
    return (token_of.reshape(EXPERTS, -1), source_of.reshape(EXPERTS, -1), used.reshape(EXPERTS, -1))

def forward(routes, tables, layer_input, gain_attn, gain_moe, w_query, w_key, w_value, w_out, w_router, w_gate, w_up, w_down):
    token_of, source_of, used = tables
    positions = jnp.arange(TOKENS, dtype=jnp.int32) % SEQ
    normed = low(rms_scale(layer_input, gain_attn))
    query = low(rotate(low_back(jnp.dot(normed, w_query, precision=HIGH)).reshape(TOKENS, HEADS, HEAD_DIM), positions))
    keys = low(rotate(low_back(jnp.dot(normed, w_key, precision=HIGH)).reshape(TOKENS, KV_HEADS, HEAD_DIM), positions))
    values = low(low_back(jnp.dot(normed, w_value, precision=HIGH))).reshape(TOKENS, KV_HEADS, HEAD_DIM)
    per_seq = jax.checkpoint(lambda parts: attend(parts[0], parts[1], parts[2]))
    heads = lax.map(per_seq, (query.reshape(N_EXPERT, SEQ, HEADS, HEAD_DIM), keys.reshape(N_EXPERT, SEQ, KV_HEADS, HEAD_DIM), values.reshape(N_EXPERT, SEQ, KV_HEADS, HEAD_DIM)))
    heads = low_back(low(heads.reshape(TOKENS, HEADS * HEAD_DIM)))
    attn = low_back(jnp.dot(heads, w_out, precision=HIGH))
    hidden_in = layer_input + attn
    mixed = low(rms_scale(hidden_in, gain_moe))
    logits = jnp.dot(mixed, w_router, precision=HIGH)
    chosen = jnp.take_along_axis(logits, routes, axis=1)
    gates = jax.nn.softmax(chosen, axis=-1)
    gates_flat = gates.reshape(-1)

    def expert_fn(parts):
        tokens_e, source_e, used_e, gate_w, up_w, down_w = parts
        rows = mixed[tokens_e]
        gate_pre = low_back(jnp.dot(rows, gate_w, precision=HIGH))
        up_pre = low_back(jnp.dot(rows, up_w, precision=HIGH))
        hidden = low(jax.nn.silu(gate_pre) * up_pre)
        result = low_back(low(jnp.dot(hidden, down_w, precision=HIGH)))
        return result * (gates_flat[source_e] * used_e.astype(jnp.float32))[:, None]
    weighted = lax.map(jax.checkpoint(expert_fn), (token_of, source_of, used, w_gate, w_up, w_down))
    moe = jnp.zeros((TOKENS, D), jnp.float32).at[token_of.reshape(-1)].add(weighted.reshape(-1, D))
    return hidden_in + moe

def reference(layer_input, routes, cotangent, gain_attn, gain_moe, w_query, w_key, w_value, w_out, w_router, w_gate, w_up, w_down):
    tables = make_tables(routes)
    floats = (layer_input.astype(jnp.float32), gain_attn.astype(jnp.float32), gain_moe.astype(jnp.float32), w_query.astype(jnp.float32), w_key.astype(jnp.float32), w_value.astype(jnp.float32), w_out.astype(jnp.float32), w_router.astype(jnp.float32), w_gate.astype(jnp.float32), w_up.astype(jnp.float32), w_down.astype(jnp.float32))
    result, pull = jax.vjp(lambda *arrays: forward(routes, tables, *arrays), *floats)
    grads = pull(cotangent.astype(jnp.float32))
    return (result.astype(jnp.bfloat16), grads[0], grads[3], grads[4], grads[5], grads[6], grads[1], grads[2], grads[7], grads[8], grads[9], grads[10])
```

```python
import functools

import jax
import jax.numpy as jnp
import numpy as np
from jax import lax
from jax.experimental import pallas as pl
from jax.experimental.pallas import tpu as pltpu
from jax.sharding import Mesh
from jax.sharding import PartitionSpec as P

AXES = ("expert_0", "expert_1", "tensor_0", "tensor_1")
EXPERT = ("expert_0", "expert_1")
TENSOR = ("tensor_0", "tensor_1")
MESH = pl.DeviceIdType.MESH
EPS = 1e-06
THETA = 10000.0
F32 = jnp.float32
BF16 = jnp.bfloat16
ROWS = 128
WIDTH = 1024
SEQ = 1024
HEAD = 64
CAP = 48
HALF = 64
NN = (((1,), (0,)), ((), ()))
NT = (((1,), (1,)), ((), ()))
TN = (((0,), (0,)), ((), ()))


def mul(a, b, dims=NN):
    return lax.dot_general(a, b, dims, preferred_element_type=F32)


def place():
    return tuple(lax.axis_index(a) for a in AXES)


def wrap(v):
    return lax.rem(v, 4)


def send(src, dst, out, arrive, device):
    return pltpu.make_async_remote_copy(
        src_ref=src, dst_ref=dst, send_sem=out, recv_sem=arrive, device_id=device, device_id_type=MESH
    )


def greet(devices):
    barrier = pltpu.get_barrier_semaphore()
    for device in devices:
        pl.semaphore_signal(barrier, inc=1, device_id=device, device_id_type=MESH)
    pl.semaphore_wait(barrier, len(devices))


def z_peers(me):
    x, y, z, c = me
    return [(x, y, wrap(z + d), c) for d in (1, 2, 3)] + [(x, y, z, 1 - c)]


def line_peers(me):
    x, y, z, c = me
    return [(wrap(x + d), y, z, c) for d in (1, 2, 3)] + [(x, wrap(y + d), z, c) for d in (1, 2, 3)]


class TensorGather:
    def __init__(self, me, slot, out, arrive):
        self.me, self.slot, self.out, self.arrive = me, slot, out, arrive

    def copy(self, k, source_z, source_c, device):
        ref = self.slot(source_z * 2 + source_c)
        return send(ref, ref, self.out.at[k], self.arrive.at[k], device)

    def start(self):
        x, y, z, c = self.me
        for d in (1, 3, 2):
            self.copy(d - 1, z, c, (x, y, wrap(z + d), c)).start()
        self.copy(3, z, c, (x, y, z, 1 - c)).start()

    def forward(self):
        x, y, z, c = self.me
        for d in (1, 3, 2):
            there = wrap(z + 4 - d)
            self.copy(d - 1, there, c, (x, y, wrap(z + d), c)).wait_recv()
            self.copy(3 + d, there, c, (x, y, z, 1 - c)).start()

    def finish(self):
        x, y, z, c = self.me
        for d in range(4):
            self.copy(3 + d, wrap(z + 4 - d), 1 - c, (x, y, z, 1 - c)).wait_recv()

    def drain(self):
        x, y, z, c = self.me
        for k in range(7):
            self.copy(k, z, c, (x, y, z, 1 - c)).wait_send()


class ExpertGather:
    def __init__(self, me, ref, out, arrive):
        self.me, self.ref, self.out, self.arrive = me, ref, out, arrive

    def upper(self, k, a, b, device):
        part = self.ref.at[a, b, pl.ds(0, HALF)]
        return send(part, part, self.out.at[k], self.arrive.at[k], device)

    def lower(self, k, a, b, device):
        part = self.ref.at[a, b, pl.ds(HALF, HALF)]
        return send(part, part, self.out.at[15 + k], self.arrive.at[15 + k], device)

    def start(self):
        x, y, z, c = self.me
        for d in (1, 3, 2):
            self.upper(d - 1, x, y, (wrap(x + d), y, z, c)).start()
            self.lower(d - 1, x, y, (x, wrap(y + d), z, c)).start()

    def own(self):
        x, y, z, c = self.me
        for d in (1, 3, 2):
            self.upper(3 + d - 1, x, y, (x, wrap(y + d), z, c)).start()
            self.lower(3 + d - 1, x, y, (wrap(x + d), y, z, c)).start()

    def forward(self):
        x, y, z, c = self.me
        for s in (1, 3, 2):
            a, b = wrap(x + 4 - s), wrap(y + 4 - s)
            self.upper(s - 1, a, y, (x, y, z, c)).wait_recv()
            for d in (1, 3, 2):
                self.upper(3 + 3 * s + d - 1, a, y, (x, wrap(y + d), z, c)).start()
            self.lower(s - 1, x, b, (x, y, z, c)).wait_recv()
            for d in (1, 3, 2):
                self.lower(3 + 3 * s + d - 1, x, b, (wrap(x + d), y, z, c)).start()

    def finish(self):
        x, y, z, c = self.me
        for s in range(4):
            for d in (1, 2, 3):
                a, b = wrap(x + 4 - s), wrap(y + 4 - d)
                self.upper(3 + 3 * s + d - 1, a, b, (x, y, z, c)).wait_recv()
                a, b = wrap(x + 4 - d), wrap(y + 4 - s)
                self.lower(3 + 3 * s + d - 1, a, b, (x, y, z, c)).wait_recv()

    def drain(self):
        x, y, z, c = self.me
        for k in range(15):
            self.upper(k, x, y, (x, y, z, c)).wait_send()
            self.lower(k, x, y, (x, y, z, c)).wait_send()


class TensorSum:
    def __init__(self, me, part, near, both, far, out, arrive):
        self.me, self.part, self.near, self.both, self.far = me, part, near, both, far
        self.out, self.arrive = out, arrive

    def to_core(self, i):
        x, y, z, c = self.me
        return send(
            self.part.at[2 * i + 1 - c], self.near.at[i], self.out.at[i], self.arrive.at[i], (x, y, z, 1 - c)
        )

    def along(self, i, k):
        x, y, z, c = self.me
        return send(self.both.at[i], self.far.at[k], self.out.at[4 + k], self.arrive.at[4 + k], (x, y, i, c))

    def paired(self, i):
        x, y, z, c = self.me
        return self.part[2 * i + c].astype(F32) + self.near[i].astype(F32)

    def combine(self, i):
        x, y, z, c = self.me
        self.to_core(i).wait_recv()
        self.both[i] = self.paired(i).astype(BF16)

        @pl.when(z != i)
        def _():
            self.along(i, wrap(i - z + 4) - 1).start()

    def total(self):
        x, y, z, c = self.me
        value = self.paired(z)
        for d in (1, 3, 2):
            self.along(z, d - 1).wait_recv()
            value += self.far[d - 1].astype(F32)
        return value

    def drain(self):
        for i in range(4):
            self.to_core(i).wait_send()
        for k in range(3):
            self.along(0, k).wait_send()


def scaled_inverse(values):
    return lax.rsqrt(jnp.mean(values * values, -1, keepdims=True) + EPS)


def lanes(rows):
    return lax.broadcasted_iota(jnp.int32, (rows, 128), 1)


def partner(values):
    lane = lanes(values.shape[0])
    forth = pltpu.roll(values, 96, 1)
    back = pltpu.roll(values, 32, 1)
    return jnp.where(lax.rem(lane, 64) < 32, forth, back)


def attend_kernel(
    input_ref, cot_ref, routes_ref, gain_attn_ref, gain_moe_ref, w_in_ref, w_out_ref, w_router_ref, cos_ref, sin_ref,
    whole_out, cot_out, query_out, keys_out, values_out, heads_out, lse_out, hidden_ref, mixed_ref, table_ref,
    whole, cot_all, part, near, both, far, pair,
    gather_out, gather_in, cot_send, cot_recv, sum_out, sum_in,
):
    me = place()
    x, y, z, c = me
    rank = z * 2 + c
    greet(z_peers(me) + line_peers(me))
    source = input_ref[...].astype(F32)
    whole[rank] = (source * scaled_inverse(source) * gain_attn_ref[...]).astype(BF16)
    gather = TensorGather(me, lambda k: whole.at[k], gather_out, gather_in)
    gather.start()
    cot_all[x, y] = cot_ref[...]
    cots = ExpertGather(me, cot_all, cot_send, cot_recv)
    cots.start()
    gather.forward()
    gather.finish()

    def project(k, _):
        at = pl.ds(pl.multiple_of(k * ROWS, ROWS), ROWS)
        block = whole[k]
        both_parts = mul(block, w_in_ref[...], NT)
        cosine, sine = cos_ref[at, :], sin_ref[at, :]
        query = both_parts[:, :128]
        query = query * cosine + partner(query) * sine
        query_out[at, :] = (query * 0.125).astype(BF16)
        rest = both_parts[:, 128:]
        low = lanes(ROWS) < HEAD
        rest = jnp.where(low, rest * cosine + partner(rest) * sine, rest)
        first = jnp.where(low, rest, 0.0)
        second = jnp.where(low, 0.0, rest)
        keys_out[0, at, :] = first.astype(BF16)
        keys_out[1, at, :] = pltpu.roll(first, HEAD, 1).astype(BF16)
        values_out[0, at, :] = pltpu.roll(second, HEAD, 1).astype(BF16)
        values_out[1, at, :] = second.astype(BF16)
        return 0

    lax.fori_loop(0, 8, project, 0)
    cots.own()
    cots.forward()
    sums = TensorSum(me, part, near, both, far, sum_out, sum_in)
    for i in range(4):
        count = (i + 1) * 256

        def attend(j, _, i=i, count=count):
            start = i * 256 + j * ROWS
            at = pl.ds(pl.multiple_of(start, ROWS), ROWS)
            query = query_out[at, :]
            row = start + lax.broadcasted_iota(jnp.int32, (ROWS, count), 0)
            allowed = lax.broadcasted_iota(jnp.int32, (ROWS, count), 1) <= row
            result, logs = jnp.zeros((ROWS, 128), F32), []
            for h in (0, 1):
                scores = mul(query, keys_out[h, :count, :], NT)
                scores = jnp.where(allowed, scores, -1e30)
                peak = jnp.max(scores, -1, keepdims=True)
                expo = jnp.exp(scores - peak)
                total = jnp.sum(expo, -1, keepdims=True)
                result += mul(expo.astype(BF16), values_out[h, :count, :]) * (1.0 / total)
                logs.append(peak + jnp.log(total))
            heads_out[at, :] = result.astype(BF16)
            lse_out[at, :] = jnp.where(lanes(ROWS) < HEAD, logs[0], logs[1])
            return 0

        lax.fori_loop(0, 2, attend, 0)

        def outward(j, _, i=i):
            at = pl.ds(pl.multiple_of(i * 256 + j * ROWS, ROWS), ROWS)
            part[2 * i + j] = mul(heads_out[at, :], w_out_ref[...]).astype(BF16)
            return 0

        lax.fori_loop(0, 2, outward, 0)
        sums.to_core(i).start()
        if i > 0:
            sums.combine(i - 1)
    sums.combine(3)
    hidden = source + sums.total()
    hidden_ref[...] = hidden
    mixed = (hidden * scaled_inverse(hidden) * gain_moe_ref[...]).astype(BF16)
    mixed_ref[...] = mixed
    logits = mul(w_router_ref[...], mixed, NT)
    expert = lax.broadcasted_iota(jnp.int32, (32, ROWS), 0)
    named = jnp.zeros((32, ROWS), F32)
    for k in range(8):
        named += jnp.where(routes_ref[k : k + 1, :] == expert, 1.0, 0.0)
    chosen = jnp.where(named > 0, logits, -1e30)
    expo = jnp.where(named > 0, jnp.exp(chosen - jnp.max(chosen, 0, keepdims=True)), 0.0)
    gates = expo / jnp.sum(expo, 0, keepdims=True)
    before = lax.broadcasted_iota(jnp.int32, (ROWS, ROWS), 0) < lax.broadcasted_iota(jnp.int32, (ROWS, ROWS), 1)
    slots = mul(named.astype(BF16), jnp.where(before, 1.0, 0.0).astype(BF16))
    pair[0] = gates
    pair[1] = jnp.where(named > 0, slots, -1.0)
    for g in range(16):
        table_ref[g] = jnp.zeros((8, ROWS), F32)
        table_ref[g, 0:2, :] = pair[0, 2 * g : 2 * g + 2, :]
        table_ref[g, 2:4, :] = pair[1, 2 * g : 2 * g + 2, :]
    cots.finish()

    def keep(k, _):
        whole_out[k] = whole[k]
        return 0

    lax.fori_loop(0, 8, keep, 0)

    def keep_cots(k, _):
        a, b = k // 4, lax.rem(k, 4)
        cot_out[a, b] = cot_all[a, b]
        return 0

    lax.fori_loop(0, 16, keep_cots, 0)
    gather.drain()
    cots.drain()
    sums.drain()


def others():
    return [(d // 4, d % 4) for d in range(1, 16)]


def shifted(me, o):
    x, y, z, c = me
    return wrap(x + o[0]), wrap(y + o[1])


class ExpertSum:
    def __init__(self, me, part, arrived, middle, last, out, arrive):
        self.me, self.part, self.arrived, self.middle, self.last = me, part, arrived, middle, last
        self.out, self.arrive = out, arrive

    def upper(self, d):
        x, y, z, c = self.me
        a = wrap(x + d)
        return send(
            self.part.at[a, :, pl.ds(0, HALF)], self.arrived.at[0, d - 1], self.out.at[d - 1],
            self.arrive.at[d - 1], (a, y, z, c),
        )

    def lower(self, d, j):
        x, y, z, c = self.me
        a, b = wrap(x + 1 + j), wrap(y + d)
        k = 3 + (d - 1) * 4 + j
        return send(
            self.part.at[a, b, pl.ds(HALF, HALF)], self.arrived.at[1, d - 1, a], self.out.at[k],
            self.arrive.at[k], (x, b, z, c),
        )

    def second(self, half, d):
        x, y, z, c = self.me
        k = 15 + half * 3 + d - 1
        device = (x, wrap(y + d), z, c) if half == 0 else (wrap(x + d), y, z, c)
        return send(
            self.middle.at[half, d - 1], self.last.at[half, d - 1], self.out.at[k], self.arrive.at[k], device
        )

    def turn(self, half):
        x, y, z, c = self.me
        for d in (1, 3, 2):
            if half == 0:
                self.upper(d).wait_recv()
            else:
                for j in range(4):
                    self.lower(d, j).wait_recv()
        for d in (1, 3, 2):
            self.middle[half, d - 1] = self.line(half, d).astype(BF16)
            self.second(half, d).start()

    def line(self, half, d):
        x, y, z, c = self.me
        if half == 0:
            b = wrap(y + d)
            value = self.part[x, b, pl.ds(0, HALF), :].astype(F32)
        else:
            b = wrap(x + d)
            value = self.part[b, y, pl.ds(HALF, HALF), :].astype(F32)
        for k in range(3):
            value += self.arrived[half, k, b].astype(F32)
        return value

    def total(self, half):
        value = self.line(half, 0)
        for d in (1, 3, 2):
            self.second(half, d).wait_recv()
            value += self.last[half, d - 1].astype(F32)
        return value

    def drain(self):
        for d in (1, 2, 3):
            self.upper(d).wait_send()
            for j in range(4):
                self.lower(d, j).wait_send()
            self.second(0, d).wait_send()
            self.second(1, d).wait_send()


def experts_kernel(
    mixed_ref, table_ref, cot_ref, shards_ref,
    grads_ref, dmix_ref, dgates_ref, y_ref,
    mixed_all, tables, weights, rows_x, rows_d, rows_g, rows_h, dx, dtab, dback,
    arrived, middle, last, grads, near, both, far,
    mix_out, mix_in, tab_out, tab_in, w_send, w_recv, sum_out, sum_in, dg_out, dg_in, gr_out, gr_in,
):
    me = place()
    x, y, z, c = me
    rank = z * 2 + c
    sides = [(*shifted(me, o), z, c) for o in others()]
    greet(z_peers(me) + sides)
    mixed_all[x, y] = mixed_ref[...]
    gather = ExpertGather(me, mixed_all, mix_out, mix_in)
    gather.start()
    weights[:, rank] = shards_ref[...]
    loads = TensorGather(me, lambda k: weights.at[:, k], w_send, w_recv)
    loads.start()
    gather.own()

    def table_copy(k, device):
        o = others()[k]
        a, b = shifted(me, o)
        return send(table_ref.at[a * 4 + b], tables.at[x, y], tab_out.at[k], tab_in.at[k], device)

    for k, device in enumerate(sides):
        table_copy(k, device).start()
    tables[x, y] = table_ref[x * 4 + y]
    gather.forward()
    loads.forward()
    gather.finish()
    for k, device in enumerate(sides):
        table_copy(k, device).wait_recv()
    loads.finish()

    sums = ExpertSum(me, dx, arrived, middle, last, sum_out, sum_in)
    slot_at = lax.broadcasted_iota(jnp.int32, (CAP, ROWS), 0).astype(F32)

    def weight(m, e):
        return weights[m * 2 + e].reshape(512, WIDTH)

    def chunk(j, _):
        a = wrap(x + 1 + j)
        base = pl.multiple_of(j * 192, 192)
        at = pl.ds(base, 192)
        picks, gate_rows = [], [[], []]
        for b in range(4):
            block = tables[a, b]
            both_picks = []
            for e in (0, 1):
                pick = jnp.where(slot_at == block[2 + e : 3 + e, :], 1.0, 0.0)
                gate_rows[e].append(jnp.sum(pick * block[e : e + 1, :], -1, keepdims=True))
                both_picks.append(pick)
            pick = jnp.concatenate(both_picks, 0)
            picks.append(pick)
            low = pick.astype(BF16)
            got = mul(low, mixed_all[a, b]).astype(BF16)
            into = pl.ds(pl.multiple_of(base + b * CAP, CAP), CAP)
            rows_x[0, into, :] = got[:CAP]
            rows_x[1, into, :] = got[CAP:]
            got = mul(low, cot_ref[a, b]).astype(BF16)
            rows_d[0, into, :] = got[:CAP]
            rows_d[1, into, :] = got[CAP:]
        dots = []
        for e in (0, 1):
            gate = jnp.concatenate(gate_rows[e], 0)
            first = mul(rows_x[e, at, :], weight(0, e), NT)
            second = mul(rows_x[e, at, :], weight(1, e), NT)
            third = mul(rows_d[e, at, :], weight(2, e), NT)
            sigma = 1.0 / (1.0 + jnp.exp(-first))
            active = first * sigma
            hidden = active * second
            dots.append(jnp.sum(third * hidden, -1, keepdims=True))
            rows_h[e, at, :] = (hidden * gate).astype(BF16)
            third = third * gate
            slope = sigma * (1.0 + first * (1.0 - sigma))
            rows_g[e, 0, at, :] = (third * second * slope).astype(BF16)
            rows_g[e, 1, at, :] = (third * active).astype(BF16)
        for b in range(4):
            for e in (0, 1):
                column = dots[e][b * CAP : (b + 1) * CAP]
                dtab[a, b, e : e + 1, :] = jnp.sum(picks[b][e * CAP : (e + 1) * CAP] * column, 0, keepdims=True)
        backs = [
            (mul(rows_g[e, 0, at, :], weight(0, e)) + mul(rows_g[e, 1, at, :], weight(1, e))).astype(BF16)
            for e in (0, 1)
        ]
        for b in range(4):
            span = slice(b * CAP, (b + 1) * CAP)
            both_rows = jnp.concatenate([backs[0][span], backs[1][span]], 0)
            dx[a, b] = mul(picks[b].astype(BF16), both_rows, TN).astype(BF16)

        @pl.when(j < 3)
        def _():
            sums.upper(1 + j).start()

        for d in (1, 3, 2):
            sums.lower(d, j).start()
        ys = [mul(rows_h[e, at, :], weight(2, e)).astype(BF16) for e in (0, 1)]
        for b in range(4):
            span = slice(b * CAP, (b + 1) * CAP)
            both_rows = jnp.concatenate([ys[0][span], ys[1][span]], 0)
            y_ref[a, b] = mul(picks[b].astype(BF16), both_rows, TN).astype(BF16)
        return 0

    for a in range(4):
        for b in range(4):
            dtab[a, b] = jnp.zeros((8, ROWS), F32)
    lax.fori_loop(0, 4, chunk, 0)

    def dgates_copy(k, device):
        a, b = shifted(me, others()[k])
        return send(dtab.at[a, b], dback.at[x, y], dg_out.at[k], dg_in.at[k], device)

    for k, device in enumerate(sides):
        dgates_copy(k, device).start()
    dback[x, y] = dtab[x, y]

    def near_copy(m, i):
        return send(
            grads.at[m, 2 * i + 1 - c], near.at[m, i], gr_out.at[m, i], gr_in.at[m, i], (x, y, z, 1 - c)
        )

    def far_copy(m, i, k):
        return send(both.at[m, i], far.at[m, k], gr_out.at[m, 4 + k], gr_in.at[m, 4 + k], (x, y, i, c))

    def weight_grad(m, _):
        e = lax.rem(m, 2)
        kind = m // 2

        @pl.when(kind < 2)
        def _():
            left = rows_g[e, jnp.minimum(kind, 1)]
            value = mul(left, rows_x[e], TN)
            grads[m] = value.astype(BF16).reshape(8, HALF, WIDTH)

        @pl.when(kind == 2)
        def _():
            value = mul(rows_h[e], rows_d[e], TN)
            grads[m] = value.astype(BF16).reshape(8, HALF, WIDTH)

        for i in range(4):
            near_copy(m, i).start()
        return 0

    def add_core(m, _):
        for i in range(4):
            near_copy(m, i).wait_recv()
            both[m, i] = (grads[m, 2 * i + c].astype(F32) + near[m, i].astype(F32)).astype(BF16)

            @pl.when(z != i)
            def _():
                far_copy(m, i, wrap(i - z + 4) - 1).start()

        return 0

    def grads_total(m, _):
        value = grads[m, 2 * z + c].astype(F32) + near[m, z].astype(F32)
        for d in (1, 3, 2):
            far_copy(m, z, d - 1).wait_recv()
            value += far[m, d - 1].astype(F32)
        grads_ref[m] = value
        return 0

    def weight_grads(m, _):
        weight_grad(m, 0)

        @pl.when(m > 0)
        def _():
            add_core(m - 1, 0)

        return 0

    lax.fori_loop(0, 6, weight_grads, 0)
    add_core(5, 0)
    sums.turn(0)
    sums.turn(1)
    dmix_ref[pl.ds(0, HALF), :] = sums.total(0)
    dmix_ref[pl.ds(HALF, HALF), :] = sums.total(1)
    lax.fori_loop(0, 6, grads_total, 0)
    for k, device in enumerate(sides):
        dgates_copy(k, device).wait_recv()
    dgates_ref[...] = dback[...]

    gather.drain()
    loads.drain()
    sums.drain()
    for k, device in enumerate(sides):
        table_copy(k, device).wait_send()
        dgates_copy(k, device).wait_send()
    for m in range(6):
        for i in range(4):
            near_copy(m, i).wait_send()
        for k in range(3):
            far_copy(m, 0, k).wait_send()


def tensor_others():
    return [(d // 2, d % 2) for d in range(1, 8)]


class ExpertTotal:
    def __init__(self, me, rows, value, arrived, mine, whole, out, arrive):
        self.me, self.rows, self.value, self.arrived = me, rows, value, arrived
        self.mine, self.whole, self.out, self.arrive = mine, whole, out, arrive

    def at(self, g):
        return (
            pl.ds(pl.multiple_of((g // 2) * self.rows, self.rows), self.rows),
            pl.ds(pl.multiple_of(lax.rem(g, 2) * 512, 512), 512),
        )

    def first(self, k):
        x, y, z, c = self.me
        a, b = shifted(self.me, others()[k])
        r, s = self.at(a * 4 + b)
        return send(self.value.at[r, s], self.arrived.at[k], self.out.at[k], self.arrive.at[k], (a, b, z, c))

    def second(self, k):
        x, y, z, c = self.me
        a, b = shifted(self.me, others()[k])
        r, s = self.at(x * 4 + y)
        return send(self.mine, self.whole.at[r, s], self.out.at[15 + k], self.arrive.at[15 + k], (a, b, z, c))

    def start(self):
        for k in range(15):
            self.first(k).start()

    def turn(self):
        x, y, z, c = self.me
        r, s = self.at(x * 4 + y)
        value = self.value[r, s].astype(F32)
        for k in range(15):
            self.first(k).wait_recv()
            value += self.arrived[k].astype(F32)
        value = value.astype(BF16)
        self.mine[...] = value
        self.whole[r, s] = value
        for k in range(15):
            self.second(k).start()

    def finish(self):
        for k in range(15):
            self.second(k).wait_recv()

    def drain(self):
        for k in range(15):
            self.first(k).wait_send()
            self.second(k).wait_send()


def norm_back(grad, values, gain):
    inverse = scaled_inverse(values)
    scaled = grad * gain
    normed = values * inverse
    inner = jnp.mean(scaled * normed, -1, keepdims=True)
    return inverse * (scaled - normed * inner), normed


def backward_kernel(
    input_ref, cot_ref, hidden_ref, mixed_ref, table_ref, dgates_ref, dmix_ref, y_ref,
    gain_attn_ref, gain_moe_ref, w_in_ref, w_out_ref, w_router_ref, cos_ref, sin_ref,
    whole_ref, query_ref, keys_ref, values_ref, heads_ref, lse_ref,
    output_ref, dinput_ref, gin_ref, gout_ref, small_ref, gain_ref,
    arrived, middle, last, dall, pair, small, small_near, small_far, small_mine, small_all,
    dheads, dkeys, dvalues, dproj, gout_value, gout_arrived, gout_mine, gout_all,
    gin_value, gin_arrived, gin_mine, gin_all, gain_near, gain_mid, gain_far, part, near, both, far,
    y_out, y_in, ag_out, ag_in, sm_out, sm_in, go_out, go_in, gi_out, gi_in, ga_out, ga_in, rs_out, rs_in,
):
    me = place()
    x, y, z, c = me
    rank = z * 2 + c
    sides = [(*shifted(me, o), z, c) for o in others()]
    mates = [(x, y, wrap(z + o[0]), lax.rem(c + o[1], 2)) for o in tensor_others()]
    greet(mates + sides)
    outs = ExpertSum(me, y_ref, arrived, middle, last, y_out, y_in)
    for d in (1, 3, 2):
        outs.upper(d).start()
        for j in range(4):
            outs.lower(d, j).start()

    for g in range(16):
        pair[0, 2 * g : 2 * g + 2, :] = table_ref[g, 0:2, :]
        pair[1, 2 * g : 2 * g + 2, :] = dgates_ref[g, 0:2, :]
    gates, dgates = pair[0], pair[1]
    dlog = (gates * (dgates - jnp.sum(gates * dgates, 0, keepdims=True))).astype(BF16)
    dmixed = dmix_ref[...] + mul(dlog, w_router_ref[...], TN)
    hidden = hidden_ref[...]
    dhidden, normed = norm_back(dmixed, hidden, gain_moe_ref[...])
    dhidden += cot_ref[...].astype(F32)
    dinput_ref[...] = dhidden
    dall[rank] = dhidden.astype(BF16)
    gather = TensorGather(me, lambda k: dall.at[k], ag_out, ag_in)
    gather.start()
    small[pl.ds(0, 32), :] = mul(dlog, mixed_ref[...])
    small[pl.ds(32, 8), :] = jnp.broadcast_to(jnp.sum(dmixed * normed, 0, keepdims=True), (8, WIDTH))

    def columns(r):
        return pl.ds(pl.multiple_of(r * 128, 128), 128)

    def small_first(k):
        to = mates[k][2] * 2 + mates[k][3]
        return send(small.at[:, columns(to)], small_near.at[k], sm_out.at[k], sm_in.at[k], mates[k])

    def small_second(k):
        return send(small_mine.at[0], small_far.at[k], sm_out.at[7 + k], sm_in.at[7 + k], sides[k])

    def small_third(k):
        return send(
            small_mine.at[1], small_all.at[:, columns(rank)], sm_out.at[22 + k], sm_in.at[22 + k], mates[k]
        )

    for k in range(7):
        small_first(k).start()
    gather.forward()
    gather.finish()

    def dheads_of(k, _):
        at = pl.ds(pl.multiple_of(k * ROWS, ROWS), ROWS)
        dheads[at, :] = mul(dall[k], w_out_ref[...], NT).astype(BF16)
        return 0

    lax.fori_loop(0, 8, dheads_of, 0)
    gout_value[...] = mul(heads_ref[...], dall[...].reshape(SEQ, WIDTH), TN).astype(BF16)
    outer = ExpertTotal(me, 16, gout_value, gout_arrived, gout_mine, gout_all, go_out, go_in)
    outer.start()
    value = small[:, columns(rank)]
    for k in range(7):
        small_first(k).wait_recv()
        value += small_near[k]
    small_mine[0] = value
    for k in range(15):
        small_second(k).start()
    outs.turn(0)
    outs.turn(1)

    for h in (0, 1):
        dkeys[h] = jnp.zeros((SEQ, 128), F32)
        dvalues[h] = jnp.zeros((SEQ, 128), F32)
    for i in range(4):
        count = (i + 1) * 256

        def attend(j, _, i=i, count=count):
            start = i * 256 + j * ROWS
            at = pl.ds(pl.multiple_of(start, ROWS), ROWS)
            query, grad = query_ref[at, :], dheads[at, :]
            product = grad.astype(F32) * heads_ref[at, :].astype(F32)
            low = lanes(ROWS) < HEAD
            row = start + lax.broadcasted_iota(jnp.int32, (ROWS, count), 0)
            allowed = lax.broadcasted_iota(jnp.int32, (ROWS, count), 1) <= row
            dquery = jnp.zeros((ROWS, 128), F32)
            for h in (0, 1):
                mine = low if h == 0 else jnp.logical_not(low)
                inner = jnp.sum(jnp.where(mine, product, 0.0), -1, keepdims=True)
                scores = mul(query, keys_ref[h, :count, :], NT)
                lse = lse_ref[at, h * HEAD : h * HEAD + 1]
                probs = jnp.where(allowed, jnp.exp(jnp.where(allowed, scores - lse, -1e30)), 0.0)
                dprobs = mul(grad, values_ref[h, :count, :], NT)
                dscores = (probs * (dprobs - inner)).astype(BF16)
                dquery += mul(dscores, keys_ref[h, :count, :])
                dkeys[h, :count, :] += mul(dscores, query, TN)
                dvalues[h, :count, :] += mul(probs.astype(BF16), grad, TN)
            dquery = dquery * 0.125
            dquery = dquery * cos_ref[at, :] - partner(dquery) * sin_ref[at, :]
            dproj[at, :128] = dquery.astype(BF16)
            return 0

        lax.fori_loop(0, 2, attend, 0)

    def undo(k, _):
        at = pl.ds(pl.multiple_of(k * ROWS, ROWS), ROWS)
        low = lanes(ROWS) < HEAD
        dkey = dkeys[0, at, :] + pltpu.roll(dkeys[1, at, :], HEAD, 1)
        dkey = jnp.where(low, dkey, 0.0)
        dkey = dkey * cos_ref[at, :] - partner(dkey) * sin_ref[at, :]
        dvalue = pltpu.roll(dvalues[0, at, :], HEAD, 1) + dvalues[1, at, :]
        dproj[at, 128:] = jnp.where(low, dkey, dvalue).astype(BF16)
        return 0

    lax.fori_loop(0, 8, undo, 0)

    sums = TensorSum(me, part, near, both, far, rs_out, rs_in)
    for i in range(4):

        def outward(j, _, i=i):
            at = pl.ds(pl.multiple_of(i * 256 + j * ROWS, ROWS), ROWS)
            part[2 * i + j] = mul(dproj[at, :], w_in_ref[...]).astype(BF16)
            return 0

        lax.fori_loop(0, 2, outward, 0)
        sums.to_core(i).start()
        if i > 0:
            sums.combine(i - 1)
    sums.combine(3)

    local = mul(dproj[...], whole_ref[...].reshape(SEQ, WIDTH), TN)
    gin_value[...] = local.astype(BF16)
    inner = ExpertTotal(me, 32, gin_value, gin_arrived, gin_mine, gin_all, gi_out, gi_in)
    inner.start()
    gain_mid[0] = jnp.broadcast_to(
        jnp.sum(local * w_in_ref[...].astype(F32), 0, keepdims=True) / gain_attn_ref[...], (8, WIDTH)
    )

    def gain_first(k):
        return send(gain_mid.at[0], gain_near.at[k], ga_out.at[k], ga_in.at[k], mates[k])

    def gain_second(k):
        return send(gain_mid.at[1], gain_far.at[k], ga_out.at[7 + k], ga_in.at[7 + k], sides[k])

    for k in range(7):
        gain_first(k).start()

    value = small_mine[0]
    for k in range(15):
        small_second(k).wait_recv()
        value += small_far[k]
    small_mine[1] = value
    small_all[:, columns(rank)] = value
    for k in range(7):
        small_third(k).start()

    outer.turn()
    for half in (0, 1):
        rows = pl.ds(half * HALF, HALF)
        output_ref[rows, :] = (hidden_ref[rows, :] + outs.total(half)).astype(BF16)

    value = gain_mid[0]
    for k in range(7):
        gain_first(k).wait_recv()
        value += gain_near[k]
    gain_mid[1] = value
    for k in range(15):
        gain_second(k).start()
    inner.turn()

    dnormed = sums.total()
    source = input_ref[...].astype(F32)
    dsource, _ = norm_back(dnormed, source, gain_attn_ref[...])
    dinput_ref[...] += dsource

    for k in range(7):
        small_third(k).wait_recv()
    small_ref[...] = small_all[...]
    outer.finish()
    gout_ref[...] = gout_all[...].astype(F32)
    value = gain_mid[1]
    for k in range(15):
        gain_second(k).wait_recv()
        value += gain_far[k]
    gain_ref[...] = value
    inner.finish()
    gin_ref[...] = gin_all[...].astype(F32)

    gather.drain()
    outs.drain()
    sums.drain()
    outer.drain()
    inner.drain()
    for k in range(7):
        small_first(k).wait_send()
        small_third(k).wait_send()
        gain_first(k).wait_send()
    for k in range(15):
        small_second(k).wait_send()
        gain_second(k).wait_send()


def call(body, inputs, outputs, scratch, number):
    semaphores = [pltpu.SemaphoreType.DMA(s) if isinstance(s, tuple) else s for s in scratch]
    return pl.pallas_call(
        body,
        out_shape=[jax.ShapeDtypeStruct(s, t) for s, t in outputs],
        in_specs=[pl.BlockSpec(memory_space=pltpu.VMEM)] * len(inputs),
        out_specs=[pl.BlockSpec(memory_space=pltpu.VMEM)] * len(outputs),
        scratch_shapes=semaphores,
        compiler_params=pltpu.CompilerParams(
            collective_id=number, has_side_effects=True, vmem_limit_bytes=60 * 1024 * 1024
        ),
    )(*inputs)


def rope_tables():
    half = HEAD // 2
    freqs = np.float32(THETA) ** (-np.arange(half, dtype=np.float32) * np.float32(2.0 / HEAD))
    angles = np.arange(SEQ, dtype=np.float32)[:, None] * freqs[None, :].astype(np.float32)
    cosine, sine = np.cos(angles).astype(np.float32), np.sin(angles).astype(np.float32)
    return np.concatenate([cosine] * 4, 1), np.concatenate([-sine, sine, -sine, sine], 1)


def per_device(
    layer_input, routes, cotangent, gain_attn, gain_moe, w_query, w_key, w_value, w_out, w_router, w_gate, w_up, w_down
):
    vmem = pltpu.VMEM
    gain_attn, gain_moe = gain_attn[None, :], gain_moe[None, :]
    w_in = jnp.concatenate([w_query.T, w_key.T, w_value.T], 0)
    router = w_router.T
    cosine, sine = (jnp.asarray(t) for t in rope_tables())
    block, seq = (ROWS, WIDTH), (8, ROWS, WIDTH)
    every = (4, 4, ROWS, WIDTH)
    whole, cots, query, keys, values, heads, lse, hidden, mixed, table = call(
        attend_kernel,
        (layer_input, cotangent, routes.T, gain_attn, gain_moe, w_in, w_out, router, cosine, sine),
        (
            (seq, BF16), (every, BF16), ((SEQ, 128), BF16), ((2, SEQ, 128), BF16), ((2, SEQ, 128), BF16),
            ((SEQ, 128), BF16), ((SEQ, 128), F32), (block, F32), (block, BF16), ((16, 8, ROWS), F32),
        ),
        (
            vmem(seq, BF16), vmem(every, BF16), vmem(seq, BF16), vmem((4, *block), BF16), vmem((4, *block), BF16),
            vmem((3, *block), BF16), vmem((2, 32, ROWS), F32),
            (7,), (7,), (30,), (30,), (7,), (7,),
        ),
        0,
    )
    shards = jnp.concatenate([w_gate.swapaxes(1, 2), w_up.swapaxes(1, 2), w_down], 0)
    strip = (HALF, WIDTH)
    grads, dmix, dgates, outs = call(
        experts_kernel,
        (mixed, table, cots, shards),
        (((6, *strip), F32), (block, F32), ((4, 4, 8, ROWS), F32), (every, BF16)),
        (
            vmem(every, BF16), vmem((4, 4, 8, ROWS), F32), vmem((6, 8, *strip), BF16),
            vmem((2, 768, WIDTH), BF16), vmem((2, 768, WIDTH), BF16), vmem((2, 2, 768, 512), BF16),
            vmem((2, 768, 512), BF16), vmem(every, BF16), vmem((4, 4, 8, ROWS), F32), vmem((4, 4, 8, ROWS), F32),
            vmem((2, 3, 4, *strip), BF16), vmem((2, 3, *strip), BF16), vmem((2, 3, *strip), BF16),
            vmem((6, 8, *strip), BF16), vmem((6, 4, *strip), BF16), vmem((6, 4, *strip), BF16),
            vmem((6, 3, *strip), BF16),
            (30,), (30,), (15,), (15,), (7,), (7,), (21,), (21,), (15,), (15,), (6, 7), (6, 7),
        ),
        1,
    )
    output, dinput, gin, gout, small, gain = call(
        backward_kernel,
        (
            layer_input, cotangent, hidden, mixed, table, dgates.reshape(16, 8, ROWS), dmix, outs,
            gain_attn, gain_moe, w_in, w_out, router, cosine, sine, whole, query, keys, values, heads, lse,
        ),
        ((block, BF16), (block, F32), ((256, WIDTH), F32), (block, F32), ((40, WIDTH), F32), ((8, WIDTH), F32)),
        (
            vmem((2, 3, 4, *strip), BF16), vmem((2, 3, *strip), BF16), vmem((2, 3, *strip), BF16), vmem(seq, BF16),
            vmem((2, 32, ROWS), F32), vmem((40, WIDTH), F32), vmem((7, 40, 128), F32), vmem((15, 40, 128), F32),
            vmem((2, 40, 128), F32), vmem((40, WIDTH), F32),
            vmem((SEQ, 128), BF16), vmem((2, SEQ, 128), F32), vmem((2, SEQ, 128), F32), vmem((SEQ, 256), BF16),
            vmem(block, BF16), vmem((15, 16, 512), BF16), vmem((16, 512), BF16), vmem(block, BF16),
            vmem((256, WIDTH), BF16), vmem((15, 32, 512), BF16), vmem((32, 512), BF16), vmem((256, WIDTH), BF16),
            vmem((7, 8, WIDTH), F32), vmem((2, 8, WIDTH), F32), vmem((15, 8, WIDTH), F32),
            vmem(seq, BF16), vmem((4, *block), BF16), vmem((4, *block), BF16), vmem((3, *block), BF16),
            (21,), (21,), (7,), (7,), (29,), (29,), (30,), (30,), (30,), (30,), (22,), (22,), (7,), (7,),
        ),
        2,
    )
    return (
        output,
        dinput,
        gin[:128].T,
        gin[128:192].T,
        gin[192:].T,
        gout,
        gain[0],
        small[32],
        small[:32].T,
        grads[0:2].swapaxes(1, 2),
        grads[2:4].swapaxes(1, 2),
        grads[4:6],
    )


def solution(mesh):
    split = Mesh(mesh.devices.reshape(4, 4, 4, 2), AXES)
    in_specs = (
        P(AXES, None),
        P(AXES, None),
        P(AXES, None),
        P(),
        P(),
        P(None, TENSOR),
        P(None, TENSOR),
        P(None, TENSOR),
        P(TENSOR, None),
        P(),
        P(EXPERT, None, TENSOR),
        P(EXPERT, None, TENSOR),
        P(EXPERT, TENSOR, None),
    )
    out_specs = (
        P(AXES, None),
        P(AXES, None),
        P(None, TENSOR),
        P(None, TENSOR),
        P(None, TENSOR),
        P(TENSOR, None),
        P(),
        P(),
        P(),
        P(EXPERT, None, TENSOR),
        P(EXPERT, None, TENSOR),
        P(EXPERT, TENSOR, None),
    )
    return jax.shard_map(per_device, mesh=split, in_specs=in_specs, out_specs=out_specs, check_vma=False)
```

```python
import functools

import jax
import jax.numpy as jnp
import numpy as np
from jax import lax
from jax.experimental import pallas as pl
from jax.experimental.pallas import tpu as pltpu
from jax.sharding import Mesh
from jax.sharding import PartitionSpec as P

AXES = ("expert_0", "expert_1", "tensor_0", "tensor_1")
EXPERT = ("expert_0", "expert_1")
TENSOR = ("tensor_0", "tensor_1")
MESH = pl.DeviceIdType.MESH
EPS = 1e-06
THETA = 10000.0
F32 = jnp.float32
BF16 = jnp.bfloat16
ROWS = 128
WIDTH = 1024
SEQ = 1024
HEAD = 64
CAP = 48
HALF = 64
NN = (((1,), (0,)), ((), ()))
NT = (((1,), (1,)), ((), ()))
TN = (((0,), (0,)), ((), ()))


def mul(a, b, dims=NN):
    return lax.dot_general(a, b, dims, preferred_element_type=F32)


def place():
    return tuple(lax.axis_index(a) for a in AXES)


def wrap(v):
    return lax.rem(v, 4)


def send(src, dst, out, arrive, device):
    return pltpu.make_async_remote_copy(
        src_ref=src, dst_ref=dst, send_sem=out, recv_sem=arrive, device_id=device, device_id_type=MESH
    )


def greet(devices):
    barrier = pltpu.get_barrier_semaphore()
    for device in devices:
        pl.semaphore_signal(barrier, inc=1, device_id=device, device_id_type=MESH)
    pl.semaphore_wait(barrier, len(devices))


def z_peers(me):
    x, y, z, c = me
    return [(x, y, wrap(z + d), c) for d in (1, 2, 3)] + [(x, y, z, 1 - c)]


def line_peers(me):
    x, y, z, c = me
    return [(wrap(x + d), y, z, c) for d in (1, 2, 3)] + [(x, wrap(y + d), z, c) for d in (1, 2, 3)]


SHIFTS = (0, 3, 1, 2)


class TensorGather:
    def __init__(self, me, slot, out, arrive, mine=None):
        self.me, self.slot, self.out, self.arrive, self.mine = me, slot, out, arrive, mine

    def copy(self, k, source_z, source_c, device, half=None, mine=None):
        ref = self.slot(source_z * 2 + source_c, half)
        return send(ref if mine is None else mine, ref, self.out.at[k], self.arrive.at[k], device)

    def start(self):
        x, y, z, c = self.me
        for n, d in ((0, 1), (1, 3)):
            self.copy(n, z, c, (x, y, wrap(z + d), c), mine=self.mine).start()
        self.copy(4, z, c, (x, y, z, 1 - c), mine=self.mine).start()

    def forward(self):
        x, y, z, c = self.me
        for n, d in ((0, 1), (1, 3)):
            there = wrap(z + 4 - d)
            self.copy(n, there, c, (x, y, z, 1 - c)).wait_recv()
            self.copy(2 + n, there, c, (x, y, wrap(z + d), c), half=n).start()
            self.copy(5 + n, there, c, (x, y, z, 1 - c)).start()

    def opposite(self):
        x, y, z, c = self.me
        for n in (0, 1):
            self.copy(2 + n, wrap(z + 2), c, (x, y, z, 1 - c), half=n).wait_recv()
        self.copy(7, wrap(z + 2), c, (x, y, z, 1 - c)).start()

    def finish(self):
        x, y, z, c = self.me
        for k, d in ((4, 0), (5, 1), (6, 3), (7, 2)):
            self.copy(k, wrap(z + 4 - d), 1 - c, (x, y, z, 1 - c)).wait_recv()

    def drain(self):
        x, y, z, c = self.me
        for k in range(8):
            self.copy(k, z, c, (x, y, z, 1 - c), half=k - 2 if k in (2, 3) else None).wait_send()


class ExpertGather:
    def __init__(self, me, ref, out, arrive, mine=None):
        self.me, self.ref, self.out, self.arrive, self.mine = me, ref, out, arrive, mine

    def to(self, h, line, d):
        x, y, z, c = self.me
        return (wrap(x + d), y, z, c) if (h == 0) == (line == 1) else (x, wrap(y + d), z, c)

    def copy(self, h, k, i, j, part, device):
        x, y, z, c = self.me
        a, b = (wrap(x + i), wrap(y + j)) if h == 0 else (wrap(x + j), wrap(y + i))
        rows = pl.ds(h * HALF, HALF) if part is None else pl.ds(h * HALF + part * 32, 32)
        ref = self.ref.at[a, b, rows]
        source = self.mine.at[rows] if self.mine is not None and i == 0 and j == 0 else ref
        return send(source, ref, self.out.at[h * 20 + k], self.arrive.at[h * 20 + k], device)

    def start(self):
        for n, d in ((0, 1), (1, 3)):
            for h in (0, 1):
                self.copy(h, n, 0, 0, None, self.to(h, 1, d)).start()

    def spread(self, h, s):
        for m, d in ((0, 1), (1, 3)):
            self.copy(h, 4 + 2 * s + m, SHIFTS[s], 0, None, self.to(h, 2, d)).start()

    def own(self):
        for h in (0, 1):
            self.spread(h, 0)

    def relay(self):
        for n, d in ((0, 1), (1, 3)):
            for h in (0, 1):
                self.copy(h, n, 4 - d, 0, None, self.to(h, 1, 1)).wait_recv()
                self.copy(h, 2 + n, 4 - d, 0, n, self.to(h, 1, d)).start()
                self.spread(h, 1 + n)

    def opposite(self):
        for h in (0, 1):
            for n in (0, 1):
                self.copy(h, 2 + n, 2, 0, n, self.to(h, 1, 1)).wait_recv()
            self.spread(h, 3)

    def relay_second(self, s):
        for m, d in ((0, 1), (1, 3)):
            for h in (0, 1):
                self.copy(h, 4 + 2 * s + m, SHIFTS[s], 4 - d, None, self.to(h, 1, 1)).wait_recv()
                self.copy(h, 12 + 2 * s + m, SHIFTS[s], 4 - d, m, self.to(h, 2, d)).start()

    def finish(self):
        for s in range(4):
            for m in (0, 1):
                for h in (0, 1):
                    self.copy(h, 12 + 2 * s + m, SHIFTS[s], 2, m, self.to(h, 1, 1)).wait_recv()

    def drain(self):
        for k in range(20):
            part = 0 if k in (2, 3) or k >= 12 else None
            for h in (0, 1):
                self.copy(h, k, 0, 0, part, self.to(h, 1, 1)).wait_send()


class TensorSum:
    def __init__(self, me, part, near, both, far, out, arrive):
        self.me, self.part, self.near, self.both, self.far = me, part, near, both, far
        self.out, self.arrive = out, arrive

    def to_core(self, i):
        x, y, z, c = self.me
        return send(
            self.part.at[2 * i + 1 - c], self.near.at[i], self.out.at[i], self.arrive.at[i], (x, y, z, 1 - c)
        )

    def along(self, i, k):
        x, y, z, c = self.me
        return send(self.both.at[i], self.far.at[k], self.out.at[4 + k], self.arrive.at[4 + k], (x, y, i, c))

    def paired(self, i):
        x, y, z, c = self.me
        return self.part[2 * i + c].astype(F32) + self.near[i].astype(F32)

    def combine(self, i):
        x, y, z, c = self.me
        self.to_core(i).wait_recv()
        self.both[i] = self.paired(i).astype(BF16)

        @pl.when(z != i)
        def _():
            self.along(i, wrap(i - z + 4) - 1).start()

    def total(self):
        x, y, z, c = self.me
        value = self.paired(z)
        for d in (1, 3, 2):
            self.along(z, d - 1).wait_recv()
            value += self.far[d - 1].astype(F32)
        return value

    def drain(self):
        for i in range(4):
            self.to_core(i).wait_send()
        for k in range(3):
            self.along(0, k).wait_send()


def seq_slot(ref):
    return lambda k, half: ref.at[k] if half is None else ref.at[k, pl.ds(half * HALF, HALF)]


def scaled_inverse(values):
    return lax.rsqrt(jnp.mean(values * values, -1, keepdims=True) + EPS)


def lanes(rows):
    return lax.broadcasted_iota(jnp.int32, (rows, 128), 1)


def partner(values):
    lane = lanes(values.shape[0])
    forth = pltpu.roll(values, 96, 1)
    back = pltpu.roll(values, 32, 1)
    return jnp.where(lax.rem(lane, 64) < 32, forth, back)


def attend_kernel(
    input_ref, cot_ref, routes_ref, gain_attn_ref, gain_moe_ref, w_in_ref, w_out_ref, w_router_ref, cos_ref, sin_ref, shards_ref,
    whole_out, cot_out, weights_out, query_out, keys_out, values_out, heads_out, lse_out, hidden_ref, mixed_ref, table_ref,
    whole, part, near, both, far, pair,
    gather_out, gather_in, cot_send, cot_recv, w_send, w_recv, sum_out, sum_in, local,
):
    me = place()
    x, y, z, c = me
    rank = z * 2 + c
    greet(z_peers(me) + line_peers(me))
    source = input_ref[...].astype(F32)
    whole[rank] = (source * scaled_inverse(source) * gain_attn_ref[...]).astype(BF16)
    gather = TensorGather(me, seq_slot(whole), gather_out, gather_in)
    gather.start()
    cots = ExpertGather(me, cot_out, cot_send, cot_recv, cot_ref)
    cots.start()
    keep_cot = pltpu.make_async_copy(cot_ref, cot_out.at[x, y], local.at[0])
    keep_cot.start()
    keep_shard = pltpu.make_async_copy(shards_ref, weights_out.at[:, rank], local.at[1])
    keep_shard.start()
    gather.forward()

    def slot(k, half):
        return weights_out.at[:, k] if half is None else weights_out.at[pl.ds(2 * half, 2), k]

    loads = TensorGather(me, slot, w_send, w_recv, shards_ref)
    loads.start()
    cots.own()
    gather.opposite()
    gather.finish()
    keep_whole = pltpu.make_async_copy(whole, whole_out, local.at[2])
    keep_whole.start()

    def project(k, _):
        at = pl.ds(pl.multiple_of(k * ROWS, ROWS), ROWS)
        block = whole[k]
        both_parts = mul(block, w_in_ref[...], NT)
        cosine, sine = cos_ref[at, :], sin_ref[at, :]
        query = both_parts[:, :128]
        query = query * cosine + partner(query) * sine
        query_out[at, :] = (query * 0.125).astype(BF16)
        rest = both_parts[:, 128:]
        low = lanes(ROWS) < HEAD
        rest = jnp.where(low, rest * cosine + partner(rest) * sine, rest)
        first = jnp.where(low, rest, 0.0)
        second = jnp.where(low, 0.0, rest)
        keys_out[0, at, :] = first.astype(BF16)
        keys_out[1, at, :] = pltpu.roll(first, HEAD, 1).astype(BF16)
        values_out[0, at, :] = pltpu.roll(second, HEAD, 1).astype(BF16)
        values_out[1, at, :] = second.astype(BF16)
        return 0

    lax.fori_loop(0, 8, project, 0)
    cots.relay()
    sums = TensorSum(me, part, near, both, far, sum_out, sum_in)
    for i in range(4):
        count = (i + 1) * 256

        def attend(j, _, i=i, count=count):
            start = i * 256 + j * ROWS
            at = pl.ds(pl.multiple_of(start, ROWS), ROWS)
            query = query_out[at, :]
            row = start + lax.broadcasted_iota(jnp.int32, (ROWS, count), 0)
            allowed = lax.broadcasted_iota(jnp.int32, (ROWS, count), 1) <= row
            result, logs = jnp.zeros((ROWS, 128), F32), []
            for h in (0, 1):
                scores = mul(query, keys_out[h, :count, :], NT)
                scores = jnp.where(allowed, scores, -1e30)
                peak = jnp.max(scores, -1, keepdims=True)
                expo = jnp.exp(scores - peak)
                total = jnp.sum(expo, -1, keepdims=True)
                result += mul(expo.astype(BF16), values_out[h, :count, :]) * (1.0 / total)
                logs.append(peak + jnp.log(total))
            heads_out[at, :] = result.astype(BF16)
            lse_out[at, :] = jnp.where(lanes(ROWS) < HEAD, logs[0], logs[1])
            return 0

        lax.fori_loop(0, 2, attend, 0)

        def outward(j, _, i=i):
            at = pl.ds(pl.multiple_of(i * 256 + j * ROWS, ROWS), ROWS)
            part[2 * i + j] = mul(heads_out[at, :], w_out_ref[...]).astype(BF16)
            return 0

        lax.fori_loop(0, 2, outward, 0)
        sums.to_core(i).start()
        if i > 0:
            sums.combine(i - 1)
        if i == 1:
            cots.opposite()
            cots.relay_second(0)
        if i == 2:
            cots.relay_second(1)
            loads.forward()
    sums.combine(3)
    cots.relay_second(2)
    cots.relay_second(3)
    loads.opposite()
    hidden = source + sums.total()
    hidden_ref[...] = hidden
    mixed = (hidden * scaled_inverse(hidden) * gain_moe_ref[...]).astype(BF16)
    mixed_ref[...] = mixed
    logits = mul(w_router_ref[...], mixed, NT)
    expert = lax.broadcasted_iota(jnp.int32, (32, ROWS), 0)
    named = jnp.zeros((32, ROWS), F32)
    for k in range(8):
        named += jnp.where(routes_ref[k : k + 1, :] == expert, 1.0, 0.0)
    chosen = jnp.where(named > 0, logits, -1e30)
    expo = jnp.where(named > 0, jnp.exp(chosen - jnp.max(chosen, 0, keepdims=True)), 0.0)
    gates = expo / jnp.sum(expo, 0, keepdims=True)
    before = lax.broadcasted_iota(jnp.int32, (ROWS, ROWS), 0) < lax.broadcasted_iota(jnp.int32, (ROWS, ROWS), 1)
    slots = mul(named.astype(BF16), jnp.where(before, 1.0, 0.0).astype(BF16))
    pair[0] = gates
    pair[1] = jnp.where(named > 0, slots, -1.0)
    for g in range(16):
        table_ref[g] = jnp.zeros((8, ROWS), F32)
        table_ref[g, 0:2, :] = pair[0, 2 * g : 2 * g + 2, :]
        table_ref[g, 2:4, :] = pair[1, 2 * g : 2 * g + 2, :]
    cots.finish()
    loads.finish()
    keep_cot.wait()
    keep_shard.wait()
    keep_whole.wait()
    gather.drain()
    cots.drain()
    loads.drain()
    sums.drain()


def others():
    return [(d // 4, d % 4) for d in range(1, 16)]


def shifted(me, o):
    x, y, z, c = me
    return wrap(x + o[0]), wrap(y + o[1])


class ExpertSum:
    def __init__(self, me, part, arrived, middle, last, out, arrive, own=None):
        self.own = own
        self.me, self.part, self.arrived, self.middle, self.last = me, part, arrived, middle, last
        self.out, self.arrive = out, arrive

    def upper(self, d):
        x, y, z, c = self.me
        a = wrap(x + d)
        return send(
            self.part.at[a, :, pl.ds(0, HALF)], self.arrived.at[0, d - 1], self.out.at[d - 1],
            self.arrive.at[d - 1], (a, y, z, c),
        )

    def lower(self, d, j):
        x, y, z, c = self.me
        a, b = wrap(x + 1 + j), wrap(y + d)
        k = 3 + (d - 1) * 4 + j
        return send(
            self.part.at[a, b, pl.ds(HALF, HALF)], self.arrived.at[1, d - 1, a], self.out.at[k],
            self.arrive.at[k], (x, b, z, c),
        )

    def second(self, half, d):
        x, y, z, c = self.me
        k = 15 + half * 3 + d - 1
        device = (x, wrap(y + d), z, c) if half == 0 else (wrap(x + d), y, z, c)
        return send(
            self.middle.at[half, d - 1], self.last.at[half, d - 1], self.out.at[k], self.arrive.at[k], device
        )

    def turn(self, half):
        x, y, z, c = self.me
        for d in (1, 3, 2):
            if half == 0:
                self.upper(d).wait_recv()
            else:
                for j in range(4):
                    self.lower(d, j).wait_recv()
        for d in (1, 3, 2):
            self.middle[half, d - 1] = self.line(half, d).astype(BF16)
            self.second(half, d).start()

    def line(self, half, d):
        x, y, z, c = self.me
        b = wrap((y if half == 0 else x) + d)
        if self.own is not None:
            value = self.own[half, b].astype(F32)
        elif half == 0:
            value = self.part[x, b, pl.ds(0, HALF), :].astype(F32)
        else:
            value = self.part[b, y, pl.ds(HALF, HALF), :].astype(F32)
        for k in range(3):
            value += self.arrived[half, k, b].astype(F32)
        return value

    def total(self, half):
        value = self.line(half, 0)
        for d in (1, 3, 2):
            self.second(half, d).wait_recv()
            value += self.last[half, d - 1].astype(F32)
        return value

    def drain(self):
        for d in (1, 2, 3):
            self.upper(d).wait_send()
            for j in range(4):
                self.lower(d, j).wait_send()
            self.second(0, d).wait_send()
            self.second(1, d).wait_send()


def experts_kernel(
    mixed_ref, table_ref, cot_in, shards_ref, weights_in,
    grads_ref, dmix_ref, dgates_ref, y_out, paired_out,
    y_ref, cot_ref, mixed_all, tables, weights, rows_x, rows_d, rows_g, rows_h, dx, dtab, dback,
    arrived, middle, last, grads, near, both, far,
    mix_out, mix_in, tab_out, tab_in, w_send, w_recv, sum_out, sum_in, dg_out, dg_in, gr_out, gr_in, local,
):
    me = place()
    x, y, z, c = me
    rank = z * 2 + c
    sides = [(*shifted(me, o), z, c) for o in others()]
    greet(z_peers(me) + sides)
    mixed_all[x, y] = mixed_ref[...]
    gather = ExpertGather(me, mixed_all, mix_out, mix_in)
    gather.start()
    weights[pl.ds(4, 2), rank] = shards_ref[...]

    def down_slot(k, half):
        return weights.at[pl.ds(4, 2), k] if half is None else weights.at[4 + half, k]

    loads = TensorGather(me, down_slot, w_send, w_recv)
    loads.start()
    fetch_cots = pltpu.make_async_copy(cot_in, cot_ref, local.at[0])
    fetch_cots.start()
    fetch_weights = pltpu.make_async_copy(weights_in, weights.at[pl.ds(0, 4)], local.at[1])
    fetch_weights.start()
    gather.own()

    def table_copy(k, device):
        o = others()[k]
        a, b = shifted(me, o)
        return send(table_ref.at[a * 4 + b], tables.at[x, y], tab_out.at[k], tab_in.at[k], device)

    for k, device in enumerate(sides):
        table_copy(k, device).start()
    tables[x, y] = table_ref[x * 4 + y]
    gather.relay()
    gather.relay_second(0)
    loads.forward()
    gather.opposite()
    gather.relay_second(1)
    gather.relay_second(2)
    loads.opposite()
    gather.relay_second(3)
    for k, device in enumerate(sides):
        table_copy(k, device).wait_recv()
    loads.finish()
    fetch_cots.wait()
    fetch_weights.wait()
    gather.finish()

    sums = ExpertSum(me, dx, arrived, middle, last, sum_out, sum_in)
    slot_at = lax.broadcasted_iota(jnp.int32, (CAP, ROWS), 0).astype(F32)

    def weight(m, e):
        return weights[m * 2 + e].reshape(512, WIDTH)

    def chunk(j, _):
        a = wrap(x + 1 + j)
        base = pl.multiple_of(j * 192, 192)
        at = pl.ds(base, 192)
        picks, gate_rows = [], [[], []]
        for b in range(4):
            block = tables[a, b]
            both_picks = []
            for e in (0, 1):
                pick = jnp.where(slot_at == block[2 + e : 3 + e, :], 1.0, 0.0)
                gate_rows[e].append(jnp.sum(pick * block[e : e + 1, :], -1, keepdims=True))
                both_picks.append(pick)
            pick = jnp.concatenate(both_picks, 0)
            picks.append(pick)
            low = pick.astype(BF16)
            got = mul(low, mixed_all[a, b]).astype(BF16)
            into = pl.ds(pl.multiple_of(base + b * CAP, CAP), CAP)
            rows_x[0, into, :] = got[:CAP]
            rows_x[1, into, :] = got[CAP:]
            got = mul(low, cot_ref[a, b]).astype(BF16)
            rows_d[0, into, :] = got[:CAP]
            rows_d[1, into, :] = got[CAP:]
        dots = []
        for e in (0, 1):
            gate = jnp.concatenate(gate_rows[e], 0)
            first = mul(rows_x[e, at, :], weight(0, e), NT)
            second = mul(rows_x[e, at, :], weight(1, e), NT)
            third = mul(rows_d[e, at, :], weight(2, e), NT)
            sigma = 1.0 / (1.0 + jnp.exp(-first))
            active = first * sigma
            hidden = active * second
            dots.append(jnp.sum(third * hidden, -1, keepdims=True))
            rows_h[e, at, :] = (hidden * gate).astype(BF16)
            third = third * gate
            slope = sigma * (1.0 + first * (1.0 - sigma))
            rows_g[e, 0, at, :] = (third * second * slope).astype(BF16)
            rows_g[e, 1, at, :] = (third * active).astype(BF16)
        for b in range(4):
            for e in (0, 1):
                column = dots[e][b * CAP : (b + 1) * CAP]
                dtab[a, b, e : e + 1, :] = jnp.sum(picks[b][e * CAP : (e + 1) * CAP] * column, 0, keepdims=True)
        backs = [
            (mul(rows_g[e, 0, at, :], weight(0, e)) + mul(rows_g[e, 1, at, :], weight(1, e))).astype(BF16)
            for e in (0, 1)
        ]
        for b in range(4):
            span = slice(b * CAP, (b + 1) * CAP)
            both_rows = jnp.concatenate([backs[0][span], backs[1][span]], 0)
            dx[a, b] = mul(picks[b].astype(BF16), both_rows, TN).astype(BF16)

        @pl.when(j < 3)
        def _():
            sums.upper(1 + j).start()

        for d in (1, 3, 2):
            sums.lower(d, j).start()
        ys = [mul(rows_h[e, at, :], weight(2, e)).astype(BF16) for e in (0, 1)]
        for b in range(4):
            span = slice(b * CAP, (b + 1) * CAP)
            both_rows = jnp.concatenate([ys[0][span], ys[1][span]], 0)
            y_ref[a, b] = mul(picks[b].astype(BF16), both_rows, TN).astype(BF16)
        pltpu.make_async_copy(y_ref.at[a], y_out.at[a], local.at[2 + j]).start()
        return 0

    for a in range(4):
        for b in range(4):
            dtab[a, b] = jnp.zeros((8, ROWS), F32)
    lax.fori_loop(0, 4, chunk, 0)

    def dgates_copy(k, device):
        a, b = shifted(me, others()[k])
        return send(dtab.at[a, b], dback.at[x, y], dg_out.at[k], dg_in.at[k], device)

    for k, device in enumerate(sides):
        dgates_copy(k, device).start()
    dback[x, y] = dtab[x, y]

    def near_copy(m, i):
        return send(
            grads.at[m, 2 * i + 1 - c], near.at[m, i], gr_out.at[m, i], gr_in.at[m, i], (x, y, z, 1 - c)
        )

    def far_copy(m, i, k):
        return send(both.at[m, i], far.at[m, k], gr_out.at[m, 4 + k], gr_in.at[m, 4 + k], (x, y, i, c))

    def weight_grad(m, _):
        e = lax.rem(m, 2)
        kind = m // 2

        @pl.when(kind < 2)
        def _():
            left = rows_g[e, jnp.minimum(kind, 1)]
            value = mul(left, rows_x[e], TN)
            grads[m] = value.astype(BF16).reshape(8, HALF, WIDTH)

        @pl.when(kind == 2)
        def _():
            value = mul(rows_h[e], rows_d[e], TN)
            grads[m] = value.astype(BF16).reshape(8, HALF, WIDTH)

        for i in range(4):
            near_copy(m, i).start()
        return 0

    def add_core(m, _):
        for i in range(4):
            near_copy(m, i).wait_recv()
            both[m, i] = (grads[m, 2 * i + c].astype(F32) + near[m, i].astype(F32)).astype(BF16)

            @pl.when((z != i) & (m < 3))
            def _():
                far_copy(m, i, wrap(i - z + 4) - 1).start()

        return 0

    def grads_total(m, _):
        value = grads[m, 2 * z + c].astype(F32) + near[m, z].astype(F32)
        for d in (1, 3, 2):
            far_copy(m, z, d - 1).wait_recv()
            value += far[m, d - 1].astype(F32)
        grads_ref[m] = value
        return 0

    def weight_grads(m, _):
        weight_grad(m, 0)

        @pl.when(m > 0)
        def _():
            add_core(m - 1, 0)

        return 0

    lax.fori_loop(0, 6, weight_grads, 0)
    add_core(5, 0)
    keep_paired = pltpu.make_async_copy(both.at[pl.ds(3, 3)], paired_out, local.at[6])
    keep_paired.start()
    sums.turn(0)
    sums.turn(1)
    dmix_ref[pl.ds(0, HALF), :] = sums.total(0)
    dmix_ref[pl.ds(HALF, HALF), :] = sums.total(1)
    lax.fori_loop(0, 3, grads_total, 0)
    for k, device in enumerate(sides):
        dgates_copy(k, device).wait_recv()
    dgates_ref[...] = dback[...]

    gather.drain()
    loads.drain()
    sums.drain()
    for k, device in enumerate(sides):
        table_copy(k, device).wait_send()
        dgates_copy(k, device).wait_send()
    for m in range(6):
        for i in range(4):
            near_copy(m, i).wait_send()
        if m < 3:
            for k in range(3):
                far_copy(m, 0, k).wait_send()
    keep_paired.wait()
    for j in range(4):
        a = wrap(x + 1 + j)
        pltpu.make_async_copy(y_ref.at[a], y_out.at[a], local.at[2 + j]).wait()


def tensor_others():
    return [(d // 2, d % 2) for d in range(1, 8)]


class ExpertTotal:
    def __init__(self, me, rows, value, arrived, mine, whole, out, arrive):
        self.me, self.rows, self.value, self.arrived = me, rows, value, arrived
        self.mine, self.whole, self.out, self.arrive = mine, whole, out, arrive

    def at(self, g):
        return (
            pl.ds(pl.multiple_of((g // 2) * self.rows, self.rows), self.rows),
            pl.ds(pl.multiple_of(lax.rem(g, 2) * 512, 512), 512),
        )

    def first(self, k):
        x, y, z, c = self.me
        a, b = shifted(self.me, others()[k])
        r, s = self.at(a * 4 + b)
        return send(self.value.at[r, s], self.arrived.at[k], self.out.at[k], self.arrive.at[k], (a, b, z, c))

    def second(self, k):
        x, y, z, c = self.me
        a, b = shifted(self.me, others()[k])
        r, s = self.at(x * 4 + y)
        return send(self.mine, self.whole.at[r, s], self.out.at[15 + k], self.arrive.at[15 + k], (a, b, z, c))

    def start(self):
        for k in range(15):
            self.first(k).start()

    def turn(self):
        x, y, z, c = self.me
        r, s = self.at(x * 4 + y)
        value = self.value[r, s].astype(F32)
        for k in range(15):
            self.first(k).wait_recv()
            value += self.arrived[k].astype(F32)
        value = value.astype(BF16)
        self.mine[...] = value
        self.whole[r, s] = value
        for k in range(15):
            self.second(k).start()

    def finish(self):
        for k in range(15):
            self.second(k).wait_recv()

    def drain(self):
        for k in range(15):
            self.first(k).wait_send()
            self.second(k).wait_send()


def norm_back(grad, values, gain):
    inverse = scaled_inverse(values)
    scaled = grad * gain
    normed = values * inverse
    inner = jnp.mean(scaled * normed, -1, keepdims=True)
    return inverse * (scaled - normed * inner), normed


def backward_kernel(
    input_ref, cot_ref, hidden_ref, mixed_ref, table_ref, dgates_ref, dmix_ref, y_ref, paired_ref,
    gain_attn_ref, gain_moe_ref, w_in_ref, w_out_ref, w_router_ref, cos_ref, sin_ref,
    whole_in, query_ref, keys_ref, values_ref, heads_ref, lse_ref,
    output_ref, dinput_ref, gin_ref, gout_ref, small_ref, gain_ref, grads_ref,
    whole_ref, y_own, pair_own, pair_far, probs_0, probs_1, probs_2, probs_3,
    arrived, middle, last, dall, pair, small, small_near, small_far, small_mine, small_all,
    dheads, dkeys, dvalues, dproj, gout_value, gout_arrived, gout_mine, gout_all,
    gin_value, gin_arrived, gin_mine, gin_all, gain_near, gain_mid, gain_far, part, near, both, far,
    y_out, y_in, ag_out, ag_in, sm_out, sm_in, go_out, go_in, gi_out, gi_in, ga_out, ga_in, rs_out, rs_in, pr_out, pr_in, local,
):
    me = place()
    x, y, z, c = me
    rank = z * 2 + c
    sides = [(*shifted(me, o), z, c) for o in others()]
    mates = [(x, y, wrap(z + o[0]), lax.rem(c + o[1], 2)) for o in tensor_others()]
    greet(mates + sides)
    outs = ExpertSum(me, y_ref, arrived, middle, last, y_out, y_in, y_own)
    fetches = [
        pltpu.make_async_copy(y_ref.at[x, :, pl.ds(0, HALF)], y_own.at[0], local.at[0]),
        pltpu.make_async_copy(y_ref.at[:, y, pl.ds(HALF, HALF)], y_own.at[1], local.at[1]),
        pltpu.make_async_copy(whole_in, whole_ref, local.at[2]),
        pltpu.make_async_copy(paired_ref.at[:, z], pair_own, local.at[3]),
    ]
    for fetch in fetches:
        fetch.start()
    for d in (1, 3, 2):
        outs.upper(d).start()
        for j in range(4):
            outs.lower(d, j).start()

    for g in range(16):
        pair[0, 2 * g : 2 * g + 2, :] = table_ref[g, 0:2, :]
        pair[1, 2 * g : 2 * g + 2, :] = dgates_ref[g, 0:2, :]
    gates, dgates = pair[0], pair[1]
    dlog = (gates * (dgates - jnp.sum(gates * dgates, 0, keepdims=True))).astype(BF16)
    dmixed = dmix_ref[...] + mul(dlog, w_router_ref[...], TN)
    hidden = hidden_ref[...]
    dhidden, normed = norm_back(dmixed, hidden, gain_moe_ref[...])
    dhidden += cot_ref[...].astype(F32)
    dinput_ref[...] = dhidden
    dall[rank] = dhidden.astype(BF16)
    gather = TensorGather(me, seq_slot(dall), ag_out, ag_in)
    gather.start()
    small[pl.ds(0, 32), :] = mul(dlog, mixed_ref[...])
    small[pl.ds(32, 8), :] = jnp.broadcast_to(jnp.sum(dmixed * normed, 0, keepdims=True), (8, WIDTH))

    def columns(r):
        return pl.ds(pl.multiple_of(r * 128, 128), 128)

    def small_first(k):
        to = mates[k][2] * 2 + mates[k][3]
        return send(small.at[:, columns(to)], small_near.at[k], sm_out.at[k], sm_in.at[k], mates[k])

    def small_second(k):
        return send(small_mine.at[0], small_far.at[k], sm_out.at[7 + k], sm_in.at[7 + k], sides[k])

    def small_third(k):
        return send(
            small_mine.at[1], small_all.at[:, columns(rank)], sm_out.at[22 + k], sm_in.at[22 + k], mates[k]
        )

    for k in range(7):
        small_first(k).start()
    probs_of = (probs_0, probs_1, probs_2, probs_3)

    def again(i):
        count = (i + 1) * 256

        def one(j, _):
            start = i * 256 + j * ROWS
            at = pl.ds(pl.multiple_of(start, ROWS), ROWS)
            query = query_ref[at, :]
            row = start + lax.broadcasted_iota(jnp.int32, (ROWS, count), 0)
            allowed = lax.broadcasted_iota(jnp.int32, (ROWS, count), 1) <= row
            into = pl.ds(pl.multiple_of(j * ROWS, ROWS), ROWS)
            for h in (0, 1):
                scores = mul(query, keys_ref[h, :count, :], NT)
                lse = lse_ref[at, h * HEAD : h * HEAD + 1]
                probs = jnp.exp(jnp.where(allowed, scores - lse, -1e30))
                probs_of[i][h, into, :] = probs.astype(BF16)
            return 0

        lax.fori_loop(0, 2, one, 0)

    again(3)
    again(2)
    gather.forward()

    def pair_copy(d):
        i = wrap(z + d)
        return send(paired_ref.at[:, i], pair_far.at[d - 1], pr_out.at[d - 1], pr_in.at[d - 1], (x, y, i, c))

    for d in (1, 3, 2):
        pair_copy(d).start()
    again(1)
    again(0)
    gather.opposite()
    gather.finish()
    for fetch in fetches:
        fetch.wait()

    def dheads_of(k, _):
        at = pl.ds(pl.multiple_of(k * ROWS, ROWS), ROWS)
        dheads[at, :] = mul(dall[k], w_out_ref[...], NT).astype(BF16)
        return 0

    lax.fori_loop(0, 8, dheads_of, 0)
    gout_value[...] = mul(heads_ref[...], dall[...].reshape(SEQ, WIDTH), TN).astype(BF16)
    outer = ExpertTotal(me, 16, gout_value, gout_arrived, gout_mine, gout_all, go_out, go_in)
    outer.start()
    value = small[:, columns(rank)]
    for k in range(7):
        small_first(k).wait_recv()
        value += small_near[k]
    small_mine[0] = value
    for k in range(15):
        small_second(k).start()
    for h in (0, 1):
        dkeys[h] = jnp.zeros((SEQ, 128), F32)
        dvalues[h] = jnp.zeros((SEQ, 128), F32)
    for i in range(4):
        count = (i + 1) * 256

        def attend(j, _, i=i, count=count):
            start = i * 256 + j * ROWS
            at = pl.ds(pl.multiple_of(start, ROWS), ROWS)
            query, grad = query_ref[at, :], dheads[at, :]
            product = grad.astype(F32) * heads_ref[at, :].astype(F32)
            low = lanes(ROWS) < HEAD
            taken = pl.ds(pl.multiple_of(j * ROWS, ROWS), ROWS)
            dquery = jnp.zeros((ROWS, 128), F32)
            for h in (0, 1):
                mine = low if h == 0 else jnp.logical_not(low)
                inner = jnp.sum(jnp.where(mine, product, 0.0), -1, keepdims=True)
                probs = probs_of[i][h, taken, :]
                dprobs = mul(grad, values_ref[h, :count, :], NT)
                dscores = (probs.astype(F32) * (dprobs - inner)).astype(BF16)
                dquery += mul(dscores, keys_ref[h, :count, :])
                dkeys[h, :count, :] += mul(dscores, query, TN)
                dvalues[h, :count, :] += mul(probs, grad, TN)
            dquery = dquery * 0.125
            dquery = dquery * cos_ref[at, :] - partner(dquery) * sin_ref[at, :]
            dproj[at, :128] = dquery.astype(BF16)
            return 0

        lax.fori_loop(0, 2, attend, 0)
        if i == 0:
            outs.turn(0)
        if i == 1:
            outs.turn(1)
        if i == 2:
            outer.turn()

    def undo(k, _):
        at = pl.ds(pl.multiple_of(k * ROWS, ROWS), ROWS)
        low = lanes(ROWS) < HEAD
        dkey = dkeys[0, at, :] + pltpu.roll(dkeys[1, at, :], HEAD, 1)
        dkey = jnp.where(low, dkey, 0.0)
        dkey = dkey * cos_ref[at, :] - partner(dkey) * sin_ref[at, :]
        dvalue = pltpu.roll(dvalues[0, at, :], HEAD, 1) + dvalues[1, at, :]
        dproj[at, 128:] = jnp.where(low, dkey, dvalue).astype(BF16)
        return 0

    lax.fori_loop(0, 8, undo, 0)

    product = mul(dproj[...], whole_ref[...].reshape(SEQ, WIDTH), TN)
    gin_value[...] = product.astype(BF16)
    inner = ExpertTotal(me, 32, gin_value, gin_arrived, gin_mine, gin_all, gi_out, gi_in)
    inner.start()
    gain_mid[0] = jnp.broadcast_to(
        jnp.sum(product * w_in_ref[...].astype(F32), 0, keepdims=True) / gain_attn_ref[...], (8, WIDTH)
    )

    def gain_first(k):
        return send(gain_mid.at[0], gain_near.at[k], ga_out.at[k], ga_in.at[k], mates[k])

    def gain_second(k):
        return send(gain_mid.at[1], gain_far.at[k], ga_out.at[7 + k], ga_in.at[7 + k], sides[k])

    for k in range(7):
        gain_first(k).start()

    sums = TensorSum(me, part, near, both, far, rs_out, rs_in)
    for i in range(4):

        def outward(j, _, i=i):
            at = pl.ds(pl.multiple_of(i * 256 + j * ROWS, ROWS), ROWS)
            part[2 * i + j] = mul(dproj[at, :], w_in_ref[...]).astype(BF16)
            return 0

        lax.fori_loop(0, 2, outward, 0)
        sums.to_core(i).start()
        if i > 0:
            sums.combine(i - 1)
    sums.combine(3)

    value = small_mine[0]
    for k in range(15):
        small_second(k).wait_recv()
        value += small_far[k]
    small_mine[1] = value
    small_all[:, columns(rank)] = value
    for k in range(7):
        small_third(k).start()

    value = gain_mid[0]
    for k in range(7):
        gain_first(k).wait_recv()
        value += gain_near[k]
    gain_mid[1] = value
    for k in range(15):
        gain_second(k).start()
    inner.turn()
    for half in (0, 1):
        rows = pl.ds(half * HALF, HALF)
        output_ref[rows, :] = (hidden_ref[rows, :] + outs.total(half)).astype(BF16)

    dnormed = sums.total()
    source = input_ref[...].astype(F32)
    dsource, _ = norm_back(dnormed, source, gain_attn_ref[...])
    dinput_ref[...] += dsource

    for k in range(7):
        small_third(k).wait_recv()
    small_ref[...] = small_all[...]
    for d in (1, 3, 2):
        pair_copy(d).wait_recv()

    def pair_total(m, _):
        value = pair_own[m].astype(F32)
        for k in range(3):
            value += pair_far[k, m].astype(F32)
        grads_ref[m] = value
        return 0

    lax.fori_loop(0, 3, pair_total, 0)
    outer.finish()
    gout_ref[...] = gout_all[...].astype(F32)
    value = gain_mid[1]
    for k in range(15):
        gain_second(k).wait_recv()
        value += gain_far[k]
    gain_ref[...] = value
    inner.finish()
    gin_ref[...] = gin_all[...].astype(F32)

    for d in (1, 2, 3):
        pair_copy(d).wait_send()
    gather.drain()
    outs.drain()
    sums.drain()
    outer.drain()
    inner.drain()
    for k in range(7):
        small_first(k).wait_send()
        small_third(k).wait_send()
        gain_first(k).wait_send()
    for k in range(15):
        small_second(k).wait_send()
        gain_second(k).wait_send()


def call(body, inputs, outputs, scratch, number, loose_in=(), loose_out=()):
    semaphores = [pltpu.SemaphoreType.DMA(s) if isinstance(s, tuple) else s for s in scratch]
    return pl.pallas_call(
        body,
        out_shape=[jax.ShapeDtypeStruct(s, t) for s, t in outputs],
        in_specs=[pl.BlockSpec(memory_space=pl.ANY if k in loose_in else pltpu.VMEM) for k in range(len(inputs))],
        out_specs=[pl.BlockSpec(memory_space=pl.ANY if k in loose_out else pltpu.VMEM) for k in range(len(outputs))],
        scratch_shapes=semaphores,
        compiler_params=pltpu.CompilerParams(
            collective_id=number, has_side_effects=True, vmem_limit_bytes=60 * 1024 * 1024
        ),
    )(*inputs)


def rope_tables():
    half = HEAD // 2
    freqs = np.float32(THETA) ** (-np.arange(half, dtype=np.float32) * np.float32(2.0 / HEAD))
    angles = np.arange(SEQ, dtype=np.float32)[:, None] * freqs[None, :].astype(np.float32)
    cosine, sine = np.cos(angles).astype(np.float32), np.sin(angles).astype(np.float32)
    return np.concatenate([cosine] * 4, 1), np.concatenate([-sine, sine, -sine, sine], 1)


def per_device(
    layer_input, routes, cotangent, gain_attn, gain_moe, w_query, w_key, w_value, w_out, w_router, w_gate, w_up, w_down
):
    vmem = pltpu.VMEM
    gain_attn, gain_moe = gain_attn[None, :], gain_moe[None, :]
    w_in = jnp.concatenate([w_query.T, w_key.T, w_value.T], 0)
    router = w_router.T
    cosine, sine = (jnp.asarray(t) for t in rope_tables())
    block, seq = (ROWS, WIDTH), (8, ROWS, WIDTH)
    every = (4, 4, ROWS, WIDTH)
    gate_up = jnp.concatenate([w_gate.swapaxes(1, 2), w_up.swapaxes(1, 2)], 0)
    strip = (HALF, WIDTH)
    whole, cots, weights, query, keys, values, heads, lse, hidden, mixed, table = call(
        attend_kernel,
        (layer_input, cotangent, routes.T, gain_attn, gain_moe, w_in, w_out, router, cosine, sine, gate_up),
        (
            (seq, BF16), (every, BF16), ((4, 8, *strip), BF16), ((SEQ, 128), BF16), ((2, SEQ, 128), BF16),
            ((2, SEQ, 128), BF16), ((SEQ, 128), BF16), ((SEQ, 128), F32), (block, F32), (block, BF16),
            ((16, 8, ROWS), F32),
        ),
        (
            vmem(seq, BF16), vmem(seq, BF16), vmem((4, *block), BF16), vmem((4, *block), BF16),
            vmem((3, *block), BF16), vmem((2, 32, ROWS), F32),
            (8,), (8,), (40,), (40,), (8,), (8,), (7,), (7,), (3,),
        ),
        0,
        (10,),
        (0, 1, 2),
    )
    grads, dmix, dgates, outs, paired = call(
        experts_kernel,
        (mixed, table, cots, w_down, weights),
        (((3, *strip), F32), (block, F32), ((4, 4, 8, ROWS), F32), (every, BF16), ((3, 4, *strip), BF16)),
        (
            vmem(every, BF16), vmem(every, BF16), vmem(every, BF16), vmem((4, 4, 8, ROWS), F32),
            vmem((6, 8, *strip), BF16),
            vmem((2, 768, WIDTH), BF16), vmem((2, 768, WIDTH), BF16), vmem((2, 2, 768, 512), BF16),
            vmem((2, 768, 512), BF16), vmem(every, BF16), vmem((4, 4, 8, ROWS), F32), vmem((4, 4, 8, ROWS), F32),
            vmem((2, 3, 4, *strip), BF16), vmem((2, 3, *strip), BF16), vmem((2, 3, *strip), BF16),
            vmem((6, 8, *strip), BF16), vmem((6, 4, *strip), BF16), vmem((6, 4, *strip), BF16),
            vmem((3, 3, *strip), BF16),
            (40,), (40,), (15,), (15,), (8,), (8,), (21,), (21,), (15,), (15,), (6, 7), (6, 7), (7,),
        ),
        1,
        (2, 4),
        (3, 4),
    )
    output, dinput, gin, gout, small, gain, more = call(
        backward_kernel,
        (
            layer_input, cotangent, hidden, mixed, table, dgates.reshape(16, 8, ROWS), dmix, outs, paired,
            gain_attn, gain_moe, w_in, w_out, router, cosine, sine, whole, query, keys, values, heads, lse,
        ),
        (
            (block, BF16), (block, F32), ((256, WIDTH), F32), (block, F32), ((40, WIDTH), F32), ((8, WIDTH), F32),
            ((3, *strip), F32),
        ),
        (
            vmem(seq, BF16), vmem((2, 4, *strip), BF16), vmem((3, *strip), BF16), vmem((3, 3, *strip), BF16),
            *(vmem((2, 256, (i + 1) * 256), BF16) for i in range(4)),
            vmem((2, 3, 4, *strip), BF16), vmem((2, 3, *strip), BF16), vmem((2, 3, *strip), BF16), vmem(seq, BF16),
            vmem((2, 32, ROWS), F32), vmem((40, WIDTH), F32), vmem((7, 40, 128), F32), vmem((15, 40, 128), F32),
            vmem((2, 40, 128), F32), vmem((40, WIDTH), F32),
            vmem((SEQ, 128), BF16), vmem((2, SEQ, 128), F32), vmem((2, SEQ, 128), F32), vmem((SEQ, 256), BF16),
            vmem(block, BF16), vmem((15, 16, 512), BF16), vmem((16, 512), BF16), vmem(block, BF16),
            vmem((256, WIDTH), BF16), vmem((15, 32, 512), BF16), vmem((32, 512), BF16), vmem((256, WIDTH), BF16),
            vmem((7, 8, WIDTH), F32), vmem((2, 8, WIDTH), F32), vmem((15, 8, WIDTH), F32),
            vmem(seq, BF16), vmem((4, *block), BF16), vmem((4, *block), BF16), vmem((3, *block), BF16),
            (21,), (21,), (8,), (8,), (29,), (29,), (30,), (30,), (30,), (30,), (22,), (22,), (7,), (7,),
            (3,), (3,), (4,),
        ),
        2,
        (7, 8, 16),
    )
    return (
        output,
        dinput,
        gin[:128].T,
        gin[128:192].T,
        gin[192:].T,
        gout,
        gain[0],
        small[32],
        small[:32].T,
        grads[0:2].swapaxes(1, 2),
        jnp.stack([grads[2], more[0]]).swapaxes(1, 2),
        more[1:3],
    )


def solution(mesh):
    split = Mesh(mesh.devices.reshape(4, 4, 4, 2), AXES)
    in_specs = (
        P(AXES, None),
        P(AXES, None),
        P(AXES, None),
        P(),
        P(),
        P(None, TENSOR),
        P(None, TENSOR),
        P(None, TENSOR),
        P(TENSOR, None),
        P(),
        P(EXPERT, None, TENSOR),
        P(EXPERT, None, TENSOR),
        P(EXPERT, TENSOR, None),
    )
    out_specs = (
        P(AXES, None),
        P(AXES, None),
        P(None, TENSOR),
        P(None, TENSOR),
        P(None, TENSOR),
        P(TENSOR, None),
        P(),
        P(),
        P(),
        P(EXPERT, None, TENSOR),
        P(EXPERT, None, TENSOR),
        P(EXPERT, TENSOR, None),
    )
    return jax.shard_map(per_device, mesh=split, in_specs=in_specs, out_specs=out_specs, check_vma=False)
```

```python
import functools

import jax
import jax.numpy as jnp
import numpy as np
from jax import lax
from jax.experimental import pallas as pl
from jax.experimental.pallas import tpu as pltpu
from jax.sharding import Mesh
from jax.sharding import PartitionSpec as P

AXES = ("expert_0", "expert_1", "tensor_0", "tensor_1")
EXPERT = ("expert_0", "expert_1")
TENSOR = ("tensor_0", "tensor_1")
MESH = pl.DeviceIdType.MESH
EPS = 1e-06
THETA = 10000.0
F32 = jnp.float32
BF16 = jnp.bfloat16
ROWS = 128
WIDTH = 1024
SEQ = 1024
HEAD = 64
CAP = 48
HALF = 64
NN = (((1,), (0,)), ((), ()))
NT = (((1,), (1,)), ((), ()))
TN = (((0,), (0,)), ((), ()))


def mul(a, b, dims=NN):
    return lax.dot_general(a, b, dims, preferred_element_type=F32)


def place():
    return tuple(lax.axis_index(a) for a in AXES)


def wrap(v):
    return lax.rem(v, 4)


def send(src, dst, out, arrive, device):
    return pltpu.make_async_remote_copy(
        src_ref=src, dst_ref=dst, send_sem=out, recv_sem=arrive, device_id=device, device_id_type=MESH
    )


def greet(devices):
    barrier = pltpu.get_barrier_semaphore()
    for device in devices:
        pl.semaphore_signal(barrier, inc=1, device_id=device, device_id_type=MESH)
    pl.semaphore_wait(barrier, len(devices))


def z_peers(me):
    x, y, z, c = me
    return [(x, y, wrap(z + d), c) for d in (1, 2, 3)] + [(x, y, z, 1 - c)]


def line_peers(me):
    x, y, z, c = me
    return [(wrap(x + d), y, z, c) for d in (1, 2, 3)] + [(x, wrap(y + d), z, c) for d in (1, 2, 3)]


SHIFTS = (0, 3, 1, 2)


class TensorGather:
    def __init__(self, me, slot, out, arrive, mine=None):
        self.me, self.slot, self.out, self.arrive, self.mine = me, slot, out, arrive, mine

    def copy(self, k, source_z, source_c, device, half=None, mine=None):
        ref = self.slot(source_z * 2 + source_c, half)
        return send(ref if mine is None else mine, ref, self.out.at[k], self.arrive.at[k], device)

    def start(self):
        x, y, z, c = self.me
        for n, d in ((0, 1), (1, 3)):
            self.copy(n, z, c, (x, y, wrap(z + d), c), mine=self.mine).start()
        self.copy(4, z, c, (x, y, z, 1 - c), mine=self.mine).start()

    def forward(self):
        x, y, z, c = self.me
        for n, d in ((0, 1), (1, 3)):
            there = wrap(z + 4 - d)
            self.copy(n, there, c, (x, y, z, 1 - c)).wait_recv()
            self.copy(2 + n, there, c, (x, y, wrap(z + d), c), half=n).start()
            self.copy(5 + n, there, c, (x, y, z, 1 - c)).start()

    def opposite(self):
        x, y, z, c = self.me
        for n in (0, 1):
            self.copy(2 + n, wrap(z + 2), c, (x, y, z, 1 - c), half=n).wait_recv()
        self.copy(7, wrap(z + 2), c, (x, y, z, 1 - c)).start()

    def finish(self):
        x, y, z, c = self.me
        for k, d in ((4, 0), (5, 1), (6, 3), (7, 2)):
            self.copy(k, wrap(z + 4 - d), 1 - c, (x, y, z, 1 - c)).wait_recv()

    def drain(self):
        x, y, z, c = self.me
        for k in range(8):
            self.copy(k, z, c, (x, y, z, 1 - c), half=k - 2 if k in (2, 3) else None).wait_send()


class ExpertGather:
    def __init__(self, me, ref, out, arrive, mine=None):
        self.me, self.ref, self.out, self.arrive, self.mine = me, ref, out, arrive, mine

    def to(self, h, line, d):
        x, y, z, c = self.me
        return (wrap(x + d), y, z, c) if (h == 0) == (line == 1) else (x, wrap(y + d), z, c)

    def copy(self, h, k, i, j, part, device):
        x, y, z, c = self.me
        a, b = (wrap(x + i), wrap(y + j)) if h == 0 else (wrap(x + j), wrap(y + i))
        rows = pl.ds(h * HALF, HALF) if part is None else pl.ds(h * HALF + part * 32, 32)
        ref = self.ref.at[a, b, rows]
        source = self.mine.at[rows] if self.mine is not None and i == 0 and j == 0 else ref
        return send(source, ref, self.out.at[h * 20 + k], self.arrive.at[h * 20 + k], device)

    def start(self):
        for n, d in ((0, 1), (1, 3)):
            for h in (0, 1):
                self.copy(h, n, 0, 0, None, self.to(h, 1, d)).start()

    def spread(self, h, s):
        for m, d in ((0, 1), (1, 3)):
            self.copy(h, 4 + 2 * s + m, SHIFTS[s], 0, None, self.to(h, 2, d)).start()

    def own(self):
        for h in (0, 1):
            self.spread(h, 0)

    def relay(self):
        for n, d in ((0, 1), (1, 3)):
            for h in (0, 1):
                self.copy(h, n, 4 - d, 0, None, self.to(h, 1, 1)).wait_recv()
                self.copy(h, 2 + n, 4 - d, 0, n, self.to(h, 1, d)).start()
                self.spread(h, 1 + n)

    def opposite(self):
        for h in (0, 1):
            for n in (0, 1):
                self.copy(h, 2 + n, 2, 0, n, self.to(h, 1, 1)).wait_recv()
            self.spread(h, 3)

    def relay_second(self, s):
        for m, d in ((0, 1), (1, 3)):
            for h in (0, 1):
                self.copy(h, 4 + 2 * s + m, SHIFTS[s], 4 - d, None, self.to(h, 1, 1)).wait_recv()
                self.copy(h, 12 + 2 * s + m, SHIFTS[s], 4 - d, m, self.to(h, 2, d)).start()

    def finish(self):
        for s in range(4):
            for m in (0, 1):
                for h in (0, 1):
                    self.copy(h, 12 + 2 * s + m, SHIFTS[s], 2, m, self.to(h, 1, 1)).wait_recv()

    def drain(self):
        for k in range(20):
            part = 0 if k in (2, 3) or k >= 12 else None
            for h in (0, 1):
                self.copy(h, k, 0, 0, part, self.to(h, 1, 1)).wait_send()


class TensorSum:
    def __init__(self, me, part, near, both, far, out, arrive):
        self.me, self.part, self.near, self.both, self.far = me, part, near, both, far
        self.out, self.arrive = out, arrive

    def to_core(self, i):
        x, y, z, c = self.me
        return send(
            self.part.at[2 * i + 1 - c], self.near.at[i], self.out.at[i], self.arrive.at[i], (x, y, z, 1 - c)
        )

    def along(self, i, k):
        x, y, z, c = self.me
        return send(self.both.at[i], self.far.at[k], self.out.at[4 + k], self.arrive.at[4 + k], (x, y, i, c))

    def paired(self, i):
        x, y, z, c = self.me
        return self.part[2 * i + c].astype(F32) + self.near[i].astype(F32)

    def combine(self, i):
        x, y, z, c = self.me
        self.to_core(i).wait_recv()
        self.both[i] = self.paired(i).astype(BF16)

        @pl.when(z != i)
        def _():
            self.along(i, wrap(i - z + 4) - 1).start()

    def total(self):
        x, y, z, c = self.me
        value = self.paired(z)
        for d in (1, 3, 2):
            self.along(z, d - 1).wait_recv()
            value += self.far[d - 1].astype(F32)
        return value

    def drain(self):
        for i in range(4):
            self.to_core(i).wait_send()
        for k in range(3):
            self.along(0, k).wait_send()


def seq_slot(ref):
    return lambda k, half: ref.at[k] if half is None else ref.at[k, pl.ds(half * HALF, HALF)]


def scaled_inverse(values):
    return lax.rsqrt(jnp.mean(values * values, -1, keepdims=True) + EPS)


def lanes(rows):
    return lax.broadcasted_iota(jnp.int32, (rows, 128), 1)


def partner(values):
    lane = lanes(values.shape[0])
    forth = pltpu.roll(values, 96, 1)
    back = pltpu.roll(values, 32, 1)
    return jnp.where(lax.rem(lane, 64) < 32, forth, back)


def attend_kernel(
    input_ref, cot_ref, routes_ref, gain_attn_ref, gain_moe_ref, w_query_ref, w_key_ref, w_value_ref,
    w_out_ref, w_router_ref, cos_ref, sin_ref, gate_ref, up_ref,
    whole_out, cot_out, weights_out, query_out, keys_out, values_out, heads_out, lse_out, hidden_ref, mixed_ref, table_ref, w_in_ref,
    shards_ref, whole, part, near, both, far, pair,
    gather_out, gather_in, cot_send, cot_recv, w_send, w_recv, sum_out, sum_in, local,
):
    me = place()
    x, y, z, c = me
    rank = z * 2 + c
    greet(z_peers(me) + line_peers(me))
    source = input_ref[...].astype(F32)
    whole[rank] = (source * scaled_inverse(source) * gain_attn_ref[...]).astype(BF16)
    gather = TensorGather(me, seq_slot(whole), gather_out, gather_in)
    gather.start()
    cots = ExpertGather(me, cot_out, cot_send, cot_recv, cot_ref)
    cots.start()
    shards_ref[pl.ds(0, 2)] = gate_ref[...]
    shards_ref[pl.ds(2, 2)] = up_ref[...]
    w_in_ref[pl.ds(0, 128), :] = w_query_ref[...].T
    w_in_ref[pl.ds(128, HEAD), :] = w_key_ref[...]
    w_in_ref[pl.ds(192, HEAD), :] = w_value_ref[...]
    keep_cot = pltpu.make_async_copy(cot_ref, cot_out.at[x, y], local.at[0])
    keep_cot.start()
    keep_shard = pltpu.make_async_copy(shards_ref, weights_out.at[:, rank], local.at[1])
    keep_shard.start()
    gather.forward()

    def slot(k, half):
        return weights_out.at[:, k] if half is None else weights_out.at[pl.ds(2 * half, 2), k]

    loads = TensorGather(me, slot, w_send, w_recv, shards_ref)
    loads.start()
    cots.own()
    gather.opposite()
    gather.finish()
    keep_whole = pltpu.make_async_copy(whole, whole_out, local.at[2])
    keep_whole.start()

    def project(k, _):
        at = pl.ds(pl.multiple_of(k * ROWS, ROWS), ROWS)
        block = whole[k]
        both_parts = mul(block, w_in_ref[...], NT)
        cosine, sine = cos_ref[at, :], sin_ref[at, :]
        query = both_parts[:, :128]
        query = query * cosine + partner(query) * sine
        query_out[at, :] = (query * 0.125).astype(BF16)
        rest = both_parts[:, 128:]
        low = lanes(ROWS) < HEAD
        rest = jnp.where(low, rest * cosine + partner(rest) * sine, rest)
        first = jnp.where(low, rest, 0.0)
        second = jnp.where(low, 0.0, rest)
        keys_out[0, at, :] = first.astype(BF16)
        keys_out[1, at, :] = pltpu.roll(first, HEAD, 1).astype(BF16)
        values_out[0, at, :] = pltpu.roll(second, HEAD, 1).astype(BF16)
        values_out[1, at, :] = second.astype(BF16)
        return 0

    lax.fori_loop(0, 8, project, 0)
    cots.relay()
    sums = TensorSum(me, part, near, both, far, sum_out, sum_in)
    for i in range(4):
        count = (i + 1) * 256

        def attend(j, _, i=i, count=count):
            start = i * 256 + j * ROWS
            at = pl.ds(pl.multiple_of(start, ROWS), ROWS)
            query = query_out[at, :]
            row = start + lax.broadcasted_iota(jnp.int32, (ROWS, count), 0)
            allowed = lax.broadcasted_iota(jnp.int32, (ROWS, count), 1) <= row
            result, logs = jnp.zeros((ROWS, 128), F32), []
            for h in (0, 1):
                scores = mul(query, keys_out[h, :count, :], NT)
                scores = jnp.where(allowed, scores, -1e30)
                peak = jnp.max(scores, -1, keepdims=True)
                expo = jnp.exp(scores - peak)
                total = jnp.sum(expo, -1, keepdims=True)
                result += mul(expo.astype(BF16), values_out[h, :count, :]) * (1.0 / total)
                logs.append(peak + jnp.log(total))
            heads_out[at, :] = result.astype(BF16)
            lse_out[at, :] = jnp.where(lanes(ROWS) < HEAD, logs[0], logs[1])
            return 0

        lax.fori_loop(0, 2, attend, 0)

        def outward(j, _, i=i):
            at = pl.ds(pl.multiple_of(i * 256 + j * ROWS, ROWS), ROWS)
            part[2 * i + j] = mul(heads_out[at, :], w_out_ref[...]).astype(BF16)
            return 0

        lax.fori_loop(0, 2, outward, 0)
        sums.to_core(i).start()
        if i > 0:
            sums.combine(i - 1)
        if i == 1:
            cots.opposite()
            cots.relay_second(0)
        if i == 2:
            cots.relay_second(1)
            loads.forward()
    sums.combine(3)
    cots.relay_second(2)
    cots.relay_second(3)
    loads.opposite()
    hidden = source + sums.total()
    hidden_ref[...] = hidden
    mixed = (hidden * scaled_inverse(hidden) * gain_moe_ref[...]).astype(BF16)
    mixed_ref[...] = mixed
    logits = mul(w_router_ref[...], mixed, NT)
    expert = lax.broadcasted_iota(jnp.int32, (32, ROWS), 0)
    named = jnp.zeros((32, ROWS), F32)
    for k in range(8):
        named += jnp.where(routes_ref[k : k + 1, :] == expert, 1.0, 0.0)
    chosen = jnp.where(named > 0, logits, -1e30)
    expo = jnp.where(named > 0, jnp.exp(chosen - jnp.max(chosen, 0, keepdims=True)), 0.0)
    gates = expo / jnp.sum(expo, 0, keepdims=True)
    before = lax.broadcasted_iota(jnp.int32, (ROWS, ROWS), 0) < lax.broadcasted_iota(jnp.int32, (ROWS, ROWS), 1)
    slots = mul(named.astype(BF16), jnp.where(before, 1.0, 0.0).astype(BF16))
    pair[0] = gates
    pair[1] = jnp.where(named > 0, slots, -1.0)
    for g in range(16):
        table_ref[g] = jnp.zeros((8, ROWS), F32)
        table_ref[g, 0:2, :] = pair[0, 2 * g : 2 * g + 2, :]
        table_ref[g, 2:4, :] = pair[1, 2 * g : 2 * g + 2, :]
    cots.finish()
    loads.finish()
    keep_cot.wait()
    keep_shard.wait()
    keep_whole.wait()
    gather.drain()
    cots.drain()
    loads.drain()
    sums.drain()


def others():
    return [(d // 4, d % 4) for d in range(1, 16)]


def shifted(me, o):
    x, y, z, c = me
    return wrap(x + o[0]), wrap(y + o[1])


class ExpertSum:
    def __init__(self, me, part, arrived, middle, last, out, arrive, own=None):
        self.own = own
        self.me, self.part, self.arrived, self.middle, self.last = me, part, arrived, middle, last
        self.out, self.arrive = out, arrive

    def upper(self, d):
        x, y, z, c = self.me
        a = wrap(x + d)
        return send(
            self.part.at[a, :, pl.ds(0, HALF)], self.arrived.at[0, d - 1], self.out.at[d - 1],
            self.arrive.at[d - 1], (a, y, z, c),
        )

    def lower(self, d, j):
        x, y, z, c = self.me
        a, b = wrap(x + 1 + j), wrap(y + d)
        k = 3 + (d - 1) * 4 + j
        return send(
            self.part.at[a, b, pl.ds(HALF, HALF)], self.arrived.at[1, d - 1, a], self.out.at[k],
            self.arrive.at[k], (x, b, z, c),
        )

    def second(self, half, d):
        x, y, z, c = self.me
        k = 15 + half * 3 + d - 1
        device = (x, wrap(y + d), z, c) if half == 0 else (wrap(x + d), y, z, c)
        return send(
            self.middle.at[half, d - 1], self.last.at[half, d - 1], self.out.at[k], self.arrive.at[k], device
        )

    def turn(self, half):
        x, y, z, c = self.me
        for d in (1, 3, 2):
            if half == 0:
                self.upper(d).wait_recv()
            else:
                for j in range(4):
                    self.lower(d, j).wait_recv()
        for d in (1, 3, 2):
            self.middle[half, d - 1] = self.line(half, d).astype(BF16)
            self.second(half, d).start()

    def line(self, half, d):
        x, y, z, c = self.me
        b = wrap((y if half == 0 else x) + d)
        if self.own is not None:
            value = self.own[half, b].astype(F32)
        elif half == 0:
            value = self.part[x, b, pl.ds(0, HALF), :].astype(F32)
        else:
            value = self.part[b, y, pl.ds(HALF, HALF), :].astype(F32)
        for k in range(3):
            value += self.arrived[half, k, b].astype(F32)
        return value

    def total(self, half):
        value = self.line(half, 0)
        for d in (1, 3, 2):
            self.second(half, d).wait_recv()
            value += self.last[half, d - 1].astype(F32)
        return value

    def drain(self):
        for d in (1, 2, 3):
            self.upper(d).wait_send()
            for j in range(4):
                self.lower(d, j).wait_send()
            self.second(0, d).wait_send()
            self.second(1, d).wait_send()


def experts_kernel(
    mixed_ref, table_ref, cot_in, shards_ref, weights_in,
    grads_ref, dmix_ref, dgates_ref, y_out, paired_out,
    y_ref, cot_ref, mixed_all, tables, weights, rows_x, rows_d, rows_g, rows_h, thirds, dx, dtab, dback,
    arrived, middle, last, grads, near, both, far,
    mix_out, mix_in, tab_out, tab_in, w_send, w_recv, sum_out, sum_in, dg_out, dg_in, gr_out, gr_in, local,
):
    me = place()
    x, y, z, c = me
    rank = z * 2 + c
    sides = [(*shifted(me, o), z, c) for o in others()]
    greet(z_peers(me) + sides)
    mixed_all[x, y] = mixed_ref[...]
    gather = ExpertGather(me, mixed_all, mix_out, mix_in)
    gather.start()
    weights[pl.ds(4, 2), rank] = shards_ref[...]

    def down_slot(k, half):
        return weights.at[pl.ds(4, 2), k] if half is None else weights.at[4 + half, k]

    loads = TensorGather(me, down_slot, w_send, w_recv)
    loads.start()
    fetch_cots = pltpu.make_async_copy(cot_in, cot_ref, local.at[0])
    fetch_cots.start()
    fetch_weights = pltpu.make_async_copy(weights_in, weights.at[pl.ds(0, 4)], local.at[1])
    fetch_weights.start()
    gather.own()

    def table_copy(k, device):
        o = others()[k]
        a, b = shifted(me, o)
        return send(table_ref.at[a * 4 + b], tables.at[x, y], tab_out.at[k], tab_in.at[k], device)

    for k, device in enumerate(sides):
        table_copy(k, device).start()
    tables[x, y] = table_ref[x * 4 + y]
    slot_at = lax.broadcasted_iota(jnp.int32, (CAP, ROWS), 0).astype(F32)

    def weight(m, e):
        return weights[m * 2 + e].reshape(512, WIDTH)

    def pick_of(a, b):
        block = tables[a, b]
        return jnp.concatenate([jnp.where(slot_at == block[2 + e : 3 + e, :], 1.0, 0.0) for e in (0, 1)], 0)

    def pick_cots(j, _):
        a = wrap(x + 1 + j)
        for b in range(4):
            got = mul(pick_of(a, b).astype(BF16), cot_ref[a, b]).astype(BF16)
            into = pl.ds(pl.multiple_of(j * 192 + b * CAP, CAP), CAP)
            rows_d[0, into, :] = got[:CAP]
            rows_d[1, into, :] = got[CAP:]
        return 0

    def back_down(j, _):
        at = pl.ds(pl.multiple_of(j * 192, 192), 192)
        for e in (0, 1):
            thirds[e, at, :] = mul(rows_d[e, at, :], weight(2, e), NT)
        return 0

    gather.relay()
    loads.forward()
    gather.relay_second(0)
    gather.opposite()
    for k, device in enumerate(sides):
        table_copy(k, device).wait_recv()
    fetch_cots.wait()
    fetch_weights.wait()
    gather.relay_second(1)
    lax.fori_loop(0, 2, pick_cots, 0)
    gather.relay_second(2)
    loads.opposite()
    lax.fori_loop(2, 4, pick_cots, 0)
    gather.relay_second(3)
    loads.finish()
    lax.fori_loop(0, 4, back_down, 0)
    gather.finish()

    sums = ExpertSum(me, dx, arrived, middle, last, sum_out, sum_in)

    def chunk(j, _):
        a = wrap(x + 1 + j)
        base = pl.multiple_of(j * 192, 192)
        at = pl.ds(base, 192)
        picks, gate_rows = [], [[], []]
        for b in range(4):
            block = tables[a, b]
            both_picks = []
            for e in (0, 1):
                pick = jnp.where(slot_at == block[2 + e : 3 + e, :], 1.0, 0.0)
                gate_rows[e].append(jnp.sum(pick * block[e : e + 1, :], -1, keepdims=True))
                both_picks.append(pick)
            pick = jnp.concatenate(both_picks, 0)
            picks.append(pick)
            low = pick.astype(BF16)
            got = mul(low, mixed_all[a, b]).astype(BF16)
            into = pl.ds(pl.multiple_of(base + b * CAP, CAP), CAP)
            rows_x[0, into, :] = got[:CAP]
            rows_x[1, into, :] = got[CAP:]
        dots = []
        for e in (0, 1):
            gate = jnp.concatenate(gate_rows[e], 0)
            first = mul(rows_x[e, at, :], weight(0, e), NT)
            second = mul(rows_x[e, at, :], weight(1, e), NT)
            third = thirds[e, at, :]
            sigma = 1.0 / (1.0 + jnp.exp(-first))
            active = first * sigma
            hidden = active * second
            dots.append(jnp.sum(third * hidden, -1, keepdims=True))
            rows_h[e, at, :] = (hidden * gate).astype(BF16)
            third = third * gate
            slope = sigma * (1.0 + first * (1.0 - sigma))
            rows_g[e, 0, at, :] = (third * second * slope).astype(BF16)
            rows_g[e, 1, at, :] = (third * active).astype(BF16)
        for b in range(4):
            for e in (0, 1):
                column = dots[e][b * CAP : (b + 1) * CAP]
                dtab[a, b, e : e + 1, :] = jnp.sum(picks[b][e * CAP : (e + 1) * CAP] * column, 0, keepdims=True)
        backs = [
            (mul(rows_g[e, 0, at, :], weight(0, e)) + mul(rows_g[e, 1, at, :], weight(1, e))).astype(BF16)
            for e in (0, 1)
        ]
        for b in range(4):
            span = slice(b * CAP, (b + 1) * CAP)
            both_rows = jnp.concatenate([backs[0][span], backs[1][span]], 0)
            dx[a, b] = mul(picks[b].astype(BF16), both_rows, TN).astype(BF16)

        @pl.when(j < 3)
        def _():
            sums.upper(1 + j).start()

        for d in (1, 3, 2):
            sums.lower(d, j).start()
        return 0

    def forward_rows(j, _):
        a = wrap(x + 1 + j)
        at = pl.ds(pl.multiple_of(j * 192, 192), 192)
        ys = [mul(rows_h[e, at, :], weight(2, e)).astype(BF16) for e in (0, 1)]
        for b in range(4):
            span = slice(b * CAP, (b + 1) * CAP)
            both_rows = jnp.concatenate([ys[0][span], ys[1][span]], 0)
            y_ref[a, b] = mul(pick_of(a, b).astype(BF16), both_rows, TN).astype(BF16)
        pltpu.make_async_copy(y_ref.at[a], y_out.at[a], local.at[2 + j]).start()
        return 0

    for a in range(4):
        for b in range(4):
            dtab[a, b] = jnp.zeros((8, ROWS), F32)
    lax.fori_loop(0, 4, chunk, 0)

    def dgates_copy(k, device):
        a, b = shifted(me, others()[k])
        return send(dtab.at[a, b], dback.at[x, y], dg_out.at[k], dg_in.at[k], device)

    for k, device in enumerate(sides):
        dgates_copy(k, device).start()
    dback[x, y] = dtab[x, y]

    def near_copy(m, i):
        return send(
            grads.at[m, 2 * i + 1 - c], near.at[m, i], gr_out.at[m, i], gr_in.at[m, i], (x, y, z, 1 - c)
        )

    def far_copy(m, i, k):
        return send(both.at[m, i], far.at[m, k], gr_out.at[m, 4 + k], gr_in.at[m, 4 + k], (x, y, i, c))

    def weight_grad(m, _):
        e = lax.rem(m, 2)
        kind = m // 2

        @pl.when(kind < 2)
        def _():
            left = rows_g[e, jnp.minimum(kind, 1)]
            value = mul(left, rows_x[e], TN)
            grads[m] = value.astype(BF16).reshape(8, HALF, WIDTH)

        @pl.when(kind == 2)
        def _():
            value = mul(rows_h[e], rows_d[e], TN)
            grads[m] = value.astype(BF16).reshape(8, HALF, WIDTH)

        for i in range(4):
            near_copy(m, i).start()
        return 0

    def add_core(m, _):
        for i in range(4):
            near_copy(m, i).wait_recv()
            both[m, i] = (grads[m, 2 * i + c].astype(F32) + near[m, i].astype(F32)).astype(BF16)

            @pl.when((z != i) & (m < 3))
            def _():
                far_copy(m, i, wrap(i - z + 4) - 1).start()

        return 0

    def grads_total(m, _):
        value = grads[m, 2 * z + c].astype(F32) + near[m, z].astype(F32)
        for d in (1, 3, 2):
            far_copy(m, z, d - 1).wait_recv()
            value += far[m, d - 1].astype(F32)
        grads_ref[m] = value
        return 0

    def weight_grads(m, _):
        weight_grad(m, 0)

        @pl.when(m > 0)
        def _():
            add_core(m - 1, 0)

        return 0

    lax.fori_loop(0, 6, weight_grads, 0)
    add_core(5, 0)
    keep_paired = pltpu.make_async_copy(both.at[pl.ds(3, 3)], paired_out, local.at[6])
    keep_paired.start()
    lax.fori_loop(0, 2, forward_rows, 0)
    sums.turn(0)
    sums.turn(1)
    lax.fori_loop(2, 4, forward_rows, 0)
    dmix_ref[pl.ds(0, HALF), :] = sums.total(0)
    dmix_ref[pl.ds(HALF, HALF), :] = sums.total(1)
    lax.fori_loop(0, 3, grads_total, 0)
    for k, device in enumerate(sides):
        dgates_copy(k, device).wait_recv()
    dgates_ref[...] = dback[...]

    gather.drain()
    loads.drain()
    sums.drain()
    for k, device in enumerate(sides):
        table_copy(k, device).wait_send()
        dgates_copy(k, device).wait_send()
    for m in range(6):
        for i in range(4):
            near_copy(m, i).wait_send()
        if m < 3:
            for k in range(3):
                far_copy(m, 0, k).wait_send()
    keep_paired.wait()
    for j in range(4):
        a = wrap(x + 1 + j)
        pltpu.make_async_copy(y_ref.at[a], y_out.at[a], local.at[2 + j]).wait()


def tensor_others():
    return [(d // 2, d % 2) for d in range(1, 8)]


class ExpertTotal:
    def __init__(self, me, rows, value, arrived, mine, whole, out, arrive):
        self.me, self.rows, self.value, self.arrived = me, rows, value, arrived
        self.mine, self.whole, self.out, self.arrive = mine, whole, out, arrive

    def at(self, g):
        return (
            pl.ds(pl.multiple_of((g // 2) * self.rows, self.rows), self.rows),
            pl.ds(pl.multiple_of(lax.rem(g, 2) * 512, 512), 512),
        )

    def first(self, k):
        x, y, z, c = self.me
        a, b = shifted(self.me, others()[k])
        r, s = self.at(a * 4 + b)
        return send(self.value.at[r, s], self.arrived.at[k], self.out.at[k], self.arrive.at[k], (a, b, z, c))

    def second(self, k):
        x, y, z, c = self.me
        a, b = shifted(self.me, others()[k])
        r, s = self.at(x * 4 + y)
        return send(self.mine, self.whole.at[r, s], self.out.at[15 + k], self.arrive.at[15 + k], (a, b, z, c))

    def start(self):
        for k in range(15):
            self.first(k).start()

    def turn(self):
        x, y, z, c = self.me
        r, s = self.at(x * 4 + y)
        value = self.value[r, s].astype(F32)
        for k in range(15):
            self.first(k).wait_recv()
            value += self.arrived[k].astype(F32)
        value = value.astype(BF16)
        self.mine[...] = value
        self.whole[r, s] = value
        for k in range(15):
            self.second(k).start()

    def finish(self):
        for k in range(15):
            self.second(k).wait_recv()

    def drain(self):
        for k in range(15):
            self.first(k).wait_send()
            self.second(k).wait_send()


def norm_back(grad, values, gain):
    inverse = scaled_inverse(values)
    scaled = grad * gain
    normed = values * inverse
    inner = jnp.mean(scaled * normed, -1, keepdims=True)
    return inverse * (scaled - normed * inner), normed


def backward_kernel(
    input_ref, cot_ref, hidden_ref, mixed_ref, table_ref, dgates_ref, dmix_ref, y_ref, paired_ref,
    gain_attn_ref, gain_moe_ref, w_in_ref, w_out_ref, w_router_ref, cos_ref, sin_ref,
    whole_in, query_ref, keys_ref, values_ref, heads_ref, lse_ref,
    output_ref, dinput_ref, gin_ref, gout_ref, small_ref, gain_ref, grads_ref,
    whole_ref, y_own, pair_own, pair_far, probs_0, probs_1, probs_2, probs_3,
    arrived, middle, last, dall, pair, small, small_near, small_far, small_mine, small_all,
    dheads, dkeys, dvalues, dproj, gout_value, gout_arrived, gout_mine, gout_all,
    gin_value, gin_arrived, gin_mine, gin_all, gain_near, gain_mid, gain_far, part, near, both, far,
    y_out, y_in, ag_out, ag_in, sm_out, sm_in, go_out, go_in, gi_out, gi_in, ga_out, ga_in, rs_out, rs_in, pr_out, pr_in, local,
):
    me = place()
    x, y, z, c = me
    rank = z * 2 + c
    sides = [(*shifted(me, o), z, c) for o in others()]
    mates = [(x, y, wrap(z + o[0]), lax.rem(c + o[1], 2)) for o in tensor_others()]
    greet(mates + sides)
    outs = ExpertSum(me, y_ref, arrived, middle, last, y_out, y_in, y_own)
    fetches = [
        pltpu.make_async_copy(y_ref.at[x, :, pl.ds(0, HALF)], y_own.at[0], local.at[0]),
        pltpu.make_async_copy(y_ref.at[:, y, pl.ds(HALF, HALF)], y_own.at[1], local.at[1]),
        pltpu.make_async_copy(whole_in, whole_ref, local.at[2]),
        pltpu.make_async_copy(paired_ref.at[:, z], pair_own, local.at[3]),
    ]
    for fetch in fetches:
        fetch.start()
    for d in (1, 3, 2):
        outs.upper(d).start()
        for j in range(4):
            outs.lower(d, j).start()

    for g in range(16):
        pair[0, 2 * g : 2 * g + 2, :] = table_ref[g, 0:2, :]
        pair[1, 2 * g : 2 * g + 2, :] = dgates_ref[g, 0:2, :]
    gates, dgates = pair[0], pair[1]
    dlog = (gates * (dgates - jnp.sum(gates * dgates, 0, keepdims=True))).astype(BF16)
    dmixed = dmix_ref[...] + mul(dlog, w_router_ref[...], TN)
    hidden = hidden_ref[...]
    dhidden, normed = norm_back(dmixed, hidden, gain_moe_ref[...])
    dhidden += cot_ref[...].astype(F32)
    dinput_ref[...] = dhidden
    dall[rank] = dhidden.astype(BF16)
    gather = TensorGather(me, seq_slot(dall), ag_out, ag_in)
    gather.start()
    small[pl.ds(0, 32), :] = mul(dlog, mixed_ref[...])
    small[pl.ds(32, 8), :] = jnp.broadcast_to(jnp.sum(dmixed * normed, 0, keepdims=True), (8, WIDTH))

    def columns(r):
        return pl.ds(pl.multiple_of(r * 128, 128), 128)

    def small_first(k):
        to = mates[k][2] * 2 + mates[k][3]
        return send(small.at[:, columns(to)], small_near.at[k], sm_out.at[k], sm_in.at[k], mates[k])

    def small_second(k):
        return send(small_mine.at[0], small_far.at[k], sm_out.at[7 + k], sm_in.at[7 + k], sides[k])

    def small_third(k):
        return send(
            small_mine.at[1], small_all.at[:, columns(rank)], sm_out.at[22 + k], sm_in.at[22 + k], mates[k]
        )

    for k in range(7):
        small_first(k).start()
    probs_of = (probs_0, probs_1, probs_2, probs_3)

    def again(i):
        count = (i + 1) * 256

        def one(j, _):
            start = i * 256 + j * ROWS
            at = pl.ds(pl.multiple_of(start, ROWS), ROWS)
            query = query_ref[at, :]
            row = start + lax.broadcasted_iota(jnp.int32, (ROWS, count), 0)
            allowed = lax.broadcasted_iota(jnp.int32, (ROWS, count), 1) <= row
            into = pl.ds(pl.multiple_of(j * ROWS, ROWS), ROWS)
            for h in (0, 1):
                scores = mul(query, keys_ref[h, :count, :], NT)
                lse = lse_ref[at, h * HEAD : h * HEAD + 1]
                probs = jnp.exp(jnp.where(allowed, scores - lse, -1e30))
                probs_of[i][h, into, :] = probs.astype(BF16)
            return 0

        lax.fori_loop(0, 2, one, 0)

    again(3)
    again(2)
    gather.forward()

    def pair_copy(d):
        i = wrap(z + d)
        return send(paired_ref.at[:, i], pair_far.at[d - 1], pr_out.at[d - 1], pr_in.at[d - 1], (x, y, i, c))

    for d in (1, 3, 2):
        pair_copy(d).start()
    again(1)
    again(0)
    gather.opposite()
    gather.finish()
    for fetch in fetches:
        fetch.wait()

    def dheads_of(k, _):
        at = pl.ds(pl.multiple_of(k * ROWS, ROWS), ROWS)
        dheads[at, :] = mul(dall[k], w_out_ref[...], NT).astype(BF16)
        return 0

    lax.fori_loop(0, 8, dheads_of, 0)
    gout_value[...] = mul(heads_ref[...], dall[...].reshape(SEQ, WIDTH), TN).astype(BF16)
    outer = ExpertTotal(me, 16, gout_value, gout_arrived, gout_mine, gout_all, go_out, go_in)
    outer.start()
    value = small[:, columns(rank)]
    for k in range(7):
        small_first(k).wait_recv()
        value += small_near[k]
    small_mine[0] = value
    for k in range(15):
        small_second(k).start()
    for h in (0, 1):
        dkeys[h] = jnp.zeros((SEQ, 128), F32)
        dvalues[h] = jnp.zeros((SEQ, 128), F32)
    for i in range(4):
        count = (i + 1) * 256

        def attend(j, _, i=i, count=count):
            start = i * 256 + j * ROWS
            at = pl.ds(pl.multiple_of(start, ROWS), ROWS)
            query, grad = query_ref[at, :], dheads[at, :]
            product = grad.astype(F32) * heads_ref[at, :].astype(F32)
            low = lanes(ROWS) < HEAD
            taken = pl.ds(pl.multiple_of(j * ROWS, ROWS), ROWS)
            dquery = jnp.zeros((ROWS, 128), F32)
            for h in (0, 1):
                mine = low if h == 0 else jnp.logical_not(low)
                inner = jnp.sum(jnp.where(mine, product, 0.0), -1, keepdims=True)
                probs = probs_of[i][h, taken, :]
                dprobs = mul(grad, values_ref[h, :count, :], NT)
                dscores = (probs.astype(F32) * (dprobs - inner)).astype(BF16)
                dquery += mul(dscores, keys_ref[h, :count, :])
                dkeys[h, :count, :] += mul(dscores, query, TN)
                dvalues[h, :count, :] += mul(probs, grad, TN)
            dquery = dquery * 0.125
            dquery = dquery * cos_ref[at, :] - partner(dquery) * sin_ref[at, :]
            dproj[at, :128] = dquery.astype(BF16)
            return 0

        lax.fori_loop(0, 2, attend, 0)
        if i == 0:
            outs.turn(0)
        if i == 1:
            outs.turn(1)
        if i == 2:
            outer.turn()

    def undo(k, _):
        at = pl.ds(pl.multiple_of(k * ROWS, ROWS), ROWS)
        low = lanes(ROWS) < HEAD
        dkey = dkeys[0, at, :] + pltpu.roll(dkeys[1, at, :], HEAD, 1)
        dkey = jnp.where(low, dkey, 0.0)
        dkey = dkey * cos_ref[at, :] - partner(dkey) * sin_ref[at, :]
        dvalue = pltpu.roll(dvalues[0, at, :], HEAD, 1) + dvalues[1, at, :]
        dproj[at, 128:] = jnp.where(low, dkey, dvalue).astype(BF16)
        return 0

    lax.fori_loop(0, 8, undo, 0)

    product = mul(dproj[...], whole_ref[...].reshape(SEQ, WIDTH), TN)
    gin_value[...] = product.astype(BF16)
    inner = ExpertTotal(me, 32, gin_value, gin_arrived, gin_mine, gin_all, gi_out, gi_in)
    inner.start()
    gain_mid[0] = jnp.broadcast_to(
        jnp.sum(product * w_in_ref[...].astype(F32), 0, keepdims=True) / gain_attn_ref[...], (8, WIDTH)
    )

    def gain_first(k):
        return send(gain_mid.at[0], gain_near.at[k], ga_out.at[k], ga_in.at[k], mates[k])

    def gain_second(k):
        return send(gain_mid.at[1], gain_far.at[k], ga_out.at[7 + k], ga_in.at[7 + k], sides[k])

    for k in range(7):
        gain_first(k).start()

    sums = TensorSum(me, part, near, both, far, rs_out, rs_in)
    for i in range(4):

        def outward(j, _, i=i):
            at = pl.ds(pl.multiple_of(i * 256 + j * ROWS, ROWS), ROWS)
            part[2 * i + j] = mul(dproj[at, :], w_in_ref[...]).astype(BF16)
            return 0

        lax.fori_loop(0, 2, outward, 0)
        sums.to_core(i).start()
        if i > 0:
            sums.combine(i - 1)
    sums.combine(3)

    value = small_mine[0]
    for k in range(15):
        small_second(k).wait_recv()
        value += small_far[k]
    small_mine[1] = value
    small_all[:, columns(rank)] = value
    for k in range(7):
        small_third(k).start()

    value = gain_mid[0]
    for k in range(7):
        gain_first(k).wait_recv()
        value += gain_near[k]
    gain_mid[1] = value
    for k in range(15):
        gain_second(k).start()
    inner.turn()
    for half in (0, 1):
        rows = pl.ds(half * HALF, HALF)
        output_ref[rows, :] = (hidden_ref[rows, :] + outs.total(half)).astype(BF16)

    dnormed = sums.total()
    source = input_ref[...].astype(F32)
    dsource, _ = norm_back(dnormed, source, gain_attn_ref[...])
    dinput_ref[...] += dsource

    for k in range(7):
        small_third(k).wait_recv()
    small_ref[...] = small_all[...]
    for d in (1, 3, 2):
        pair_copy(d).wait_recv()

    def pair_total(m, _):
        value = pair_own[m].astype(F32)
        for k in range(3):
            value += pair_far[k, m].astype(F32)
        grads_ref[m] = value
        return 0

    lax.fori_loop(0, 3, pair_total, 0)
    outer.finish()
    gout_ref[...] = gout_all[...].astype(F32)
    value = gain_mid[1]
    for k in range(15):
        gain_second(k).wait_recv()
        value += gain_far[k]
    gain_ref[...] = value
    inner.finish()
    gin_ref[...] = gin_all[...].astype(F32)

    for d in (1, 2, 3):
        pair_copy(d).wait_send()
    gather.drain()
    outs.drain()
    sums.drain()
    outer.drain()
    inner.drain()
    for k in range(7):
        small_first(k).wait_send()
        small_third(k).wait_send()
        gain_first(k).wait_send()
    for k in range(15):
        small_second(k).wait_send()
        gain_second(k).wait_send()


def call(body, inputs, outputs, scratch, number, loose_in=(), loose_out=()):
    semaphores = [pltpu.SemaphoreType.DMA(s) if isinstance(s, tuple) else s for s in scratch]
    return pl.pallas_call(
        body,
        out_shape=[jax.ShapeDtypeStruct(s, t) for s, t in outputs],
        in_specs=[pl.BlockSpec(memory_space=pl.ANY if k in loose_in else pltpu.VMEM) for k in range(len(inputs))],
        out_specs=[pl.BlockSpec(memory_space=pl.ANY if k in loose_out else pltpu.VMEM) for k in range(len(outputs))],
        scratch_shapes=semaphores,
        compiler_params=pltpu.CompilerParams(
            collective_id=number, has_side_effects=True, vmem_limit_bytes=60 * 1024 * 1024
        ),
    )(*inputs)


def finish_kernel(
    small_ref, gain_ref, gin, grads, more, output_in, dinput_in, gout_in,
    query_ref, router_ref, gain_attn_ref, gain_moe_ref,
    key_out, value_out, gate_out, up_out, down_out, output_out, dinput_out, gout_out,
):
    query_ref[...] = gin[:128, :].T
    router_ref[...] = small_ref[:32, :]
    gain_moe_ref[...] = small_ref[32:33, :]
    gain_attn_ref[...] = gain_ref[0:1, :]
    key_out[...] = gin[128:192, :]
    value_out[...] = gin[192:256, :]
    gate_out[...] = grads[0:2]
    up_out[0] = grads[2]
    up_out[1] = more[0]
    down_out[...] = more[1:3]
    output_out[...] = output_in[...]
    dinput_out[...] = dinput_in[...]
    gout_out[...] = gout_in[...]


def finish(small, gain, gin, grads, more, output, dinput, gout):
    strip = (HALF, WIDTH)
    near = pl.BlockSpec(memory_space=pltpu.VMEM)
    shapes = (
        ((WIDTH, 128), F32), ((32, WIDTH), F32), ((1, WIDTH), F32), ((1, WIDTH), F32), (strip, F32), (strip, F32),
        ((2, *strip), F32), ((2, *strip), F32), ((2, *strip), F32), (output.shape, BF16), (dinput.shape, F32),
        (gout.shape, F32),
    )
    return pl.pallas_call(
        finish_kernel,
        out_shape=[jax.ShapeDtypeStruct(s, t) for s, t in shapes],
        in_specs=[near] * 8,
        out_specs=[near] * len(shapes),
        compiler_params=pltpu.CompilerParams(vmem_limit_bytes=60 * 1024 * 1024),
    )(small, gain, gin, grads, more, output, dinput, gout)


def rope_tables():
    half = HEAD // 2
    freqs = np.float32(THETA) ** (-np.arange(half, dtype=np.float32) * np.float32(2.0 / HEAD))
    angles = np.arange(SEQ, dtype=np.float32)[:, None] * freqs[None, :].astype(np.float32)
    cosine, sine = np.cos(angles).astype(np.float32), np.sin(angles).astype(np.float32)
    return np.concatenate([cosine] * 4, 1), np.concatenate([-sine, sine, -sine, sine], 1)


def per_device(
    layer_input, routes, cotangent, gain_attn, gain_moe, w_query, w_key, w_value, w_out, w_router, w_gate, w_up, w_down
):
    vmem = pltpu.VMEM
    gain_attn, gain_moe = gain_attn[None, :], gain_moe[None, :]
    router = w_router.T
    cosine, sine = (jnp.asarray(t) for t in rope_tables())
    block, seq = (ROWS, WIDTH), (8, ROWS, WIDTH)
    every = (4, 4, ROWS, WIDTH)
    strip = (HALF, WIDTH)
    whole, cots, weights, query, keys, values, heads, lse, hidden, mixed, table, w_in = call(
        attend_kernel,
        (
            layer_input, cotangent, routes.T, gain_attn, gain_moe, w_query, w_key.T, w_value.T, w_out, router,
            cosine, sine, w_gate.swapaxes(1, 2), w_up.swapaxes(1, 2),
        ),
        (
            (seq, BF16), (every, BF16), ((4, 8, *strip), BF16), ((SEQ, 128), BF16), ((2, SEQ, 128), BF16),
            ((2, SEQ, 128), BF16), ((SEQ, 128), BF16), ((SEQ, 128), F32), (block, F32), (block, BF16),
            ((16, 8, ROWS), F32), ((256, WIDTH), BF16),
        ),
        (
            vmem((4, *strip), BF16), vmem(seq, BF16), vmem(seq, BF16), vmem((4, *block), BF16), vmem((4, *block), BF16),
            vmem((3, *block), BF16), vmem((2, 32, ROWS), F32),
            (8,), (8,), (40,), (40,), (8,), (8,), (7,), (7,), (3,),
        ),
        0,
        (),
        (0, 1, 2),
    )
    grads, dmix, dgates, outs, paired = call(
        experts_kernel,
        (mixed, table, cots, w_down, weights),
        (((3, *strip), F32), (block, F32), ((4, 4, 8, ROWS), F32), (every, BF16), ((3, 4, *strip), BF16)),
        (
            vmem(every, BF16), vmem(every, BF16), vmem(every, BF16), vmem((4, 4, 8, ROWS), F32),
            vmem((6, 8, *strip), BF16),
            vmem((2, 768, WIDTH), BF16), vmem((2, 768, WIDTH), BF16), vmem((2, 2, 768, 512), BF16),
            vmem((2, 768, 512), BF16), vmem((2, 768, 512), F32), vmem(every, BF16), vmem((4, 4, 8, ROWS), F32),
            vmem((4, 4, 8, ROWS), F32),
            vmem((2, 3, 4, *strip), BF16), vmem((2, 3, *strip), BF16), vmem((2, 3, *strip), BF16),
            vmem((6, 8, *strip), BF16), vmem((6, 4, *strip), BF16), vmem((6, 4, *strip), BF16),
            vmem((3, 3, *strip), BF16),
            (40,), (40,), (15,), (15,), (8,), (8,), (21,), (21,), (15,), (15,), (6, 7), (6, 7), (7,),
        ),
        1,
        (2, 4),
        (3, 4),
    )
    output, dinput, gin, gout, small, gain, more = call(
        backward_kernel,
        (
            layer_input, cotangent, hidden, mixed, table, dgates.reshape(16, 8, ROWS), dmix, outs, paired,
            gain_attn, gain_moe, w_in, w_out, router, cosine, sine, whole, query, keys, values, heads, lse,
        ),
        (
            (block, BF16), (block, F32), ((256, WIDTH), F32), (block, F32), ((40, WIDTH), F32), ((8, WIDTH), F32),
            ((3, *strip), F32),
        ),
        (
            vmem(seq, BF16), vmem((2, 4, *strip), BF16), vmem((3, *strip), BF16), vmem((3, 3, *strip), BF16),
            *(vmem((2, 256, (i + 1) * 256), BF16) for i in range(4)),
            vmem((2, 3, 4, *strip), BF16), vmem((2, 3, *strip), BF16), vmem((2, 3, *strip), BF16), vmem(seq, BF16),
            vmem((2, 32, ROWS), F32), vmem((40, WIDTH), F32), vmem((7, 40, 128), F32), vmem((15, 40, 128), F32),
            vmem((2, 40, 128), F32), vmem((40, WIDTH), F32),
            vmem((SEQ, 128), BF16), vmem((2, SEQ, 128), F32), vmem((2, SEQ, 128), F32), vmem((SEQ, 256), BF16),
            vmem(block, BF16), vmem((15, 16, 512), BF16), vmem((16, 512), BF16), vmem(block, BF16),
            vmem((256, WIDTH), BF16), vmem((15, 32, 512), BF16), vmem((32, 512), BF16), vmem((256, WIDTH), BF16),
            vmem((7, 8, WIDTH), F32), vmem((2, 8, WIDTH), F32), vmem((15, 8, WIDTH), F32),
            vmem(seq, BF16), vmem((4, *block), BF16), vmem((4, *block), BF16), vmem((3, *block), BF16),
            (21,), (21,), (8,), (8,), (29,), (29,), (30,), (30,), (30,), (30,), (22,), (22,), (7,), (7,),
            (3,), (3,), (4,),
        ),
        2,
        (7, 8, 16),
    )
    (grad_query, grad_router, grad_attn, grad_moe, grad_key, grad_value, grad_gate, grad_up, grad_down, output, dinput,
     gout) = finish(small, gain, gin, grads, more, output, dinput, gout)
    return (
        output,
        dinput,
        grad_query,
        grad_key.T,
        grad_value.T,
        gout,
        grad_attn.reshape(-1),
        grad_moe.reshape(-1),
        grad_router.T,
        grad_gate.swapaxes(1, 2),
        grad_up.swapaxes(1, 2),
        grad_down,
    )


def solution(mesh):
    split = Mesh(mesh.devices.reshape(4, 4, 4, 2), AXES)
    in_specs = (
        P(AXES, None),
        P(AXES, None),
        P(AXES, None),
        P(),
        P(),
        P(None, TENSOR),
        P(None, TENSOR),
        P(None, TENSOR),
        P(TENSOR, None),
        P(),
        P(EXPERT, None, TENSOR),
        P(EXPERT, None, TENSOR),
        P(EXPERT, TENSOR, None),
    )
    out_specs = (
        P(AXES, None),
        P(AXES, None),
        P(None, TENSOR),
        P(None, TENSOR),
        P(None, TENSOR),
        P(TENSOR, None),
        P(),
        P(),
        P(),
        P(EXPERT, None, TENSOR),
        P(EXPERT, None, TENSOR),
        P(EXPERT, TENSOR, None),
    )
    return jax.shard_map(per_device, mesh=split, in_specs=in_specs, out_specs=out_specs, check_vma=False)
```
